512 devices in a mesh: grp: 4 (over x), row: 128 (over z, y, core).
Axes of the slice: x: 4, y: 8, z: 8, core: 2. Of those that a mesh axis runs over, the one named last changes fastest.
Arguments:
- pressure: float32 [1, 1048576], P(None, ('grp', 'row')), may hold values from -6 to 6
- mic_cycle: int32 [1, 1048576], P(None, ('grp', 'row')), may hold values from 0 to 4095, as said below
- mic_azimuth: int32 [1, 1048576], P(None, ('grp', 'row')), may hold values from 0 to 8191
- bin_index: int32 [1], replicated, may hold values from 0 to 15
- source_cell: int32 [512], replicated, may hold values from 0 to 999, as said below
Outputs:
- strengths: float32 [1, 512], P(None, 'grp')
The draws below stay inside these ranges and needn't reach their ends.
Inputs may be any that keep to these rules, and one draw needn't show every extreme that they name: `source_cell`: distinct cells of a 10 x 10 x 10 grid. `mic_cycle`: within each bin, never falling along the sample axis.
All inputs are finite; a program needn't handle non-finite values.
Results may differ from the reference program's by a relative error of at most 0.0003.
Values sent between devices are 32-bit elements; how exact they have to be, the bound alone decides.
A program may use at most 64 MiB of HBM per device.

```python
import jax
import jax.numpy as jnp
from jax import lax

S = 512
FB = 1
MD = 2048
NRING = 4096
NAZ = 8192
NBINS = 16
ROWS = 1048576


def draw_source_cell(key, part):
    key = jax.random.fold_in(key, 7)
    scores = jax.random.randint(key, (1000,), 0, 1 << 20) * 1000 + jnp.arange(1000, dtype=jnp.int32)
    scores = scores.at[0].set(-2).at[999].set(-1)
    ranked = jnp.argsort(scores, stable=True)
    return ranked[:S].astype(jnp.int32)


def draw_mic_cycle(key, part):
    key = jax.random.fold_in(key, 11)
    subkeys = jax.random.split(key, 5)
    band_count = 16
    starts = jax.random.randint(subkeys[0], (FB, band_count), 0, NRING - 256)
    widths = jax.random.randint(subkeys[1], (FB, band_count), 32, 257)
    first_pick = jax.random.randint(subkeys[2], (FB, ROWS), 0, band_count)
    second_pick = jax.random.randint(subkeys[3], (FB, ROWS), 0, band_count)
    choose = jnp.minimum(first_pick, second_pick)
    band_base = jnp.take_along_axis(starts, choose, axis=1)
    band_span = jnp.take_along_axis(widths, choose, axis=1)
    offset = jax.random.randint(subkeys[4], (FB, ROWS), 0, 1 << 20) % band_span
    cycles = band_base + offset
    cycles = cycles.at[:, 0].set(0).at[:, ROWS - 1].set(NRING - 1)
    return jnp.sort(cycles, axis=1).astype(jnp.int32)


def touch_ends(entries, rng, low, high):
    longest = entries.shape.index(max(entries.shape))
    spots = []
    for shift in (0, 1):
        where = [jax.random.randint(jax.random.fold_in(rng, axis), (), 0, length) for axis, length in enumerate(entries.shape)]
        where[longest] = (where[longest] + shift) % entries.shape[longest]
        spots.append(tuple(where))
    return entries.at[spots[0]].set(low).at[spots[1]].set(high)


def block_scale(key, dims, pieces, smallest, high):
    gain = 1.0
    for position, blocks in pieces:
        heights = jax.random.uniform(jax.random.fold_in(jax.random.fold_in(key, 6), position), (blocks,), jnp.float32, smallest / len(pieces), high / len(pieces))
        gain = gain * jnp.repeat(jnp.exp(heights), dims[position] // blocks).reshape((-1,) + (1,) * (len(dims) - 1 - position))
    return gain


def bell_draw(key, dims, deviation, reach, shards=(), kind=jnp.bfloat16):
    drawn = deviation * jax.random.normal(key, dims, jnp.float32)
    if shards:
        drawn = drawn * block_scale(key, dims, shards, -0.22, 0.18)
    return jnp.clip(drawn, -reach, reach).astype(kind)


def setup_inputs(seed: int = 0) -> dict:
    splits = jax.random.split(jax.random.key(seed), 6)
    return {
        "pressure": bell_draw(splits[0], (FB, ROWS), 1.0, 6.0, ((1, 512),), jnp.float32),
        "mic_cycle": draw_mic_cycle(jax.random.fold_in(splits[5], 71), 0),
        "mic_azimuth": touch_ends(jax.random.randint(splits[2], (FB, ROWS), 0, NAZ), jax.random.fold_in(splits[2], 1), 0, NAZ - 1).astype(jnp.int32),
        "bin_index": jax.random.randint(splits[3], (FB,), 0, NBINS).astype(jnp.int32),
        "source_cell": draw_source_cell(jax.random.fold_in(splits[5], 71), 0),
    }


ridge = 0.5
spacing = 0.08

def source_points(source_cell):
    layer_i = (source_cell // 100).astype(jnp.float32)
    layer_j = (source_cell // 10 % 10).astype(jnp.float32)
    layer_l = (source_cell % 10).astype(jnp.float32)
    return (spacing * (layer_i - 4.5), spacing * (layer_j - 4.5), spacing * (layer_l - 4.5))

def green_block(cycle_idx, azim_idx, points, wavenum):
    polar = jnp.pi * (cycle_idx.astype(jnp.float32) + 0.5) / NRING
    azimuth = 2.0 * jnp.pi * azim_idx.astype(jnp.float32) / NAZ
    mic_x = jnp.sin(polar) * jnp.cos(azimuth)
    mic_y = jnp.sin(polar) * jnp.sin(azimuth)
    mic_z = jnp.cos(polar)
    delta_x = mic_x[..., None] - points[0]
    delta_y = mic_y[..., None] - points[1]
    delta_z = mic_z[..., None] - points[2]
    dist = jnp.sqrt(delta_x * delta_x + delta_y * delta_y + delta_z * delta_z)
    return jnp.cos(wavenum[:, None, None] * dist) / dist

def solve_batch(factor, vector):
    middle = lax.linalg.triangular_solve(factor, vector[..., None], left_side=True, lower=True)
    result = lax.linalg.triangular_solve(factor, middle, left_side=True, lower=True, transpose_a=True)
    return result[..., 0]

def reference(pressure, mic_cycle, mic_azimuth, bin_index, source_cell):
    points = source_points(source_cell)
    wavenum = 1.5 * (bin_index.astype(jnp.float32) + 1.0)
    blocks = ROWS // MD

    def regroup(array):
        return jnp.moveaxis(array.reshape(FB, blocks, MD), 1, 0)

    def step(carry, items):
        gram_acc, rhs_acc = carry
        press_blk, cycle_blk, azim_blk = items
        panel = green_block(cycle_blk, azim_blk, points, wavenum)
        gram_acc = gram_acc + jnp.einsum('fms,fmt->fst', panel, panel, precision=lax.Precision.HIGHEST)
        rhs_acc = rhs_acc + jnp.einsum('fms,fm->fs', panel, press_blk, precision=lax.Precision.HIGHEST)
        return ((gram_acc, rhs_acc), None)
    start = (jnp.zeros((FB, S, S), jnp.float32), jnp.zeros((FB, S), jnp.float32))
    (gram_sum, rhs_sum), _ = lax.scan(step, start, (regroup(pressure), regroup(mic_cycle), regroup(mic_azimuth)))
    gram = gram_sum / ROWS + ridge * jnp.eye(S, dtype=jnp.float32)
    rhs = rhs_sum / jnp.sqrt(jnp.float32(ROWS))
    lower = jnp.linalg.cholesky(gram)
    return solve_batch(lower, rhs)
```

```python
import functools

import jax
import jax.numpy as jnp
import numpy as np
from jax import lax
from jax.experimental import pallas as pl
from jax.experimental.pallas import tpu as pltpu
from jax.sharding import PartitionSpec as P

F32 = jnp.float32
BF = jnp.bfloat16
S = 512
NRING = 4096
NAZ = 8192
PAIRS = [(i, j) for i in range(4) for j in range(i, 4)]

NT=(((1,),(1,)),((),()))
CHUNK=256
COS=[float(v) for v in (6.283185307179586,-41.34170224039975,81.60524927607504,-76.70585975306136,42.05869394489765)]
MAGIC=12582912.0

def split(v,n):
    parts=[]
    for _ in range(n-1):
        h=v.astype(BF); parts.append(h); v=v-h.astype(F32)
    parts.append(v.astype(BF)); return parts

def cos_turns(t, gain=None):
    y=t-((t+MAGIC)-MAGIC)
    v=0.25-jnp.abs(y)
    u=v*v
    s=COS[4]
    for c in COS[3::-1]: s=s*u+c
    return (s*v) if gain is None else s*(v*gain)

def panel_kernel(spacing, bin_ref, p_ref, cyc_ref, az_ref, src_ref, out_ref, src_scr, mic_scr, hi_scr, lo_scr):
    cell=src_ref[...].astype(F32)
    li=jnp.floor((cell+0.5)*0.01); rest=cell-100.0*li
    lj=jnp.floor((rest+0.5)*0.1); ll=rest-10.0*lj
    t=[2.0*v-9.0 for v in (li,lj,ll)]
    sq=t[0]*t[0]+t[1]*t[1]+t[2]*t[2]
    one=jnp.ones_like(sq); zero=jnp.zeros_like(sq)
    rows=[t[0]]*3+[t[1]]*3+[t[2]]*3+[sq]*3+[one]
    sT=jnp.concatenate(rows+[zero]*(128-len(rows)),axis=0)
    src_scr[...]=sT.T.astype(BF)
    half=spacing*0.5
    polar=(2*cyc_ref[...]+1).astype(F32)*(1.0/16384.0)
    azim=az_ref[...].astype(F32)*(1.0/8192.0)
    sp=cos_turns(polar-0.25); cp=cos_turns(polar)
    mic=[sp*cos_turns(azim), sp*cos_turns(azim-0.25), cp]
    mrows=[]
    for m in mic: mrows+=split(m*(-2.0*half),3)
    w=jnp.full(mic[0].shape,half*half,F32)
    mrows+=split(w,3)+[jnp.ones_like(w).astype(BF)]
    mrows=[m.astype(F32) for m in mrows]
    mrows+=[jnp.zeros_like(w)]*(16-len(mrows))
    mic_scr[...]=jnp.concatenate(mrows,axis=0).astype(BF)
    n=p_ref.shape[1]
    ph,pm=[v.astype(F32) for v in split(p_ref[...],2)]
    hi_scr[S:S+16,:]=jnp.concatenate([ph,pm]+[jnp.zeros_like(ph)]*14,axis=0).astype(BF)
    kc=1.5*(bin_ref[0].astype(F32)+1.0)*float(1/(2*np.pi))
    for c in range(n//CHUNK):
        cols=slice(c*CHUNK,(c+1)*CHUNK)
        d2=jnp.dot(src_scr[:,:16],mic_scr[:,cols],preferred_element_type=F32)
        r=lax.rsqrt(d2)
        val=cos_turns((d2*r)*kc, r)
        h=val.astype(BF)
        hi_scr[0:S,cols]=h
        lo_scr[:,cols]=(val-h.astype(F32)).astype(BF)
    H=lax.dot_general(hi_scr[...],hi_scr[0:S,:],NT,preferred_element_type=F32)
    L=lax.dot_general(hi_scr[...],lo_scr[...],NT,preferred_element_type=F32)
    nblk=0
    for i in range(4):
        for j in range(i,4):
            a=slice(128*i,128*i+128); b=slice(128*j,128*j+128)
            out_ref[128*nblk:128*nblk+128,:]=H[a,b]+L[a,b]+L[b,a].T
            nblk+=1
    r=(H[S:S+1]+L[S:S+1])+(H[S+1:S+2]+L[S+1:S+2])
    tail=jnp.concatenate([r[:,128*i:128*i+128] for i in range(4)]+[jnp.zeros((4,128),F32)],axis=0)
    out_ref[1280:1288,:]=tail
    out_ref[1288:1536,:]=jnp.zeros((248,128),F32)

def panel(spacing, p, cyc, az, b, src):
    n=p.shape[1]
    V=pl.BlockSpec(memory_space=pltpu.VMEM)
    return pl.pallas_call(functools.partial(panel_kernel,spacing),
        out_shape=jax.ShapeDtypeStruct((1536,128),F32),
        in_specs=[pl.BlockSpec(memory_space=pltpu.SMEM),V,V,V,V],out_specs=V,
        scratch_shapes=[pltpu.VMEM((S,128),BF),pltpu.VMEM((16,n),BF),pltpu.VMEM((S+16,n),BF),pltpu.VMEM((S,n),BF)],
        name="panel",compiler_params=pltpu.CompilerParams(vmem_limit_bytes=40<<20))(b,p,cyc,az,src.reshape(1,S))

MESH = pl.DeviceIdType.MESH


def reduce_kernel(nx, ny, nz, piece, in_ref, out_ref, acc_c, acc_x, acc_y, buf_c, buf_x, buf_y, buf_z,
                  send_c, recv_c, send_x, recv_x, send_y, recv_y, send_z, recv_z,
                  gsend_c, grecv_c, gsend_x, grecv_x, gsend_y, grecv_y):
    x = lax.axis_index("grp")
    row = lax.axis_index("row")
    c = lax.rem(row, 2)
    y = lax.rem(row // 2, ny)
    z = row // (2 * ny)
    def at_c(o):
        return {"row": row + lax.rem(c + o, 2) - c}
    def at_x(o):
        return {"grp": lax.rem(x + o, nx)}
    def at_y(o):
        return {"row": row + 2 * (lax.rem(y + o, ny) - y)}
    def at_z(o):
        return {"row": row + 2 * ny * (lax.rem(z + o, nz) - z)}
    partners = [at_c(1)] + [at_x(o) for o in range(1, nx)] + [at_y(o) for o in range(1, ny)]
    partners += [at_z(o) for o in range(1, nz)]
    barrier = pltpu.get_barrier_semaphore()
    for partner in partners:
        pl.semaphore_signal(barrier, inc=1, device_id=partner, device_id_type=MESH)
    pl.semaphore_wait(barrier, len(partners))

    def send(src, dst, ssem, rsem, partner):
        copy = pltpu.make_async_remote_copy(src_ref=src, dst_ref=dst, send_sem=ssem, recv_sem=rsem,
                                            device_id=partner, device_id_type=MESH)
        copy.start()
        return copy

    def rows(start, count):
        return pl.ds(pl.multiple_of(start, 8), count)

    row_y, row_x, row_c = piece, piece * ny, piece * ny * nx
    copy = send(in_ref.at[rows((1 - c) * row_c, row_c)], buf_c, send_c, recv_c, at_c(1))
    copy.wait()
    acc_c[...] = in_ref[rows(c * row_c, row_c), :] + buf_c[...]
    copies = [send(acc_c.at[rows(lax.rem(x + o, nx) * row_x, row_x)], buf_x.at[o - 1],
                   send_x.at[o - 1], recv_x.at[o - 1], at_x(o)) for o in range(1, nx)]
    for copy in copies:
        copy.wait()
    total = acc_c[rows(x * row_x, row_x), :]
    for o in range(1, nx):
        total = total + buf_x[o - 1]
    acc_x[...] = total
    copies = [send(acc_x.at[rows(lax.rem(y + o, ny) * row_y, row_y)], buf_y.at[o - 1],
                   send_y.at[o - 1], recv_y.at[o - 1], at_y(o)) for o in range(1, ny)]
    for copy in copies:
        copy.wait()
    total = acc_x[rows(y * row_y, row_y), :]
    for o in range(1, ny):
        total = total + buf_y[o - 1]
    acc_y[...] = total
    buf_z[z] = total
    copies = [send(acc_y, buf_z.at[z], send_z.at[o - 1], recv_z.at[o - 1], at_z(o)) for o in range(1, nz)]
    for copy in copies:
        copy.wait()
    total = buf_z[0]
    for o in range(1, nz):
        total = total + buf_z[o]
    mine = out_ref.at[rows(c * row_c + x * row_x + y * row_y, row_y)]
    mine[...] = total
    copies = [send(mine, mine, gsend_y.at[o - 1], grecv_y.at[o - 1], at_y(o)) for o in range(1, ny)]
    for copy in copies:
        copy.wait()
    mine = out_ref.at[rows(c * row_c + x * row_x, row_x)]
    copies = [send(mine, mine, gsend_x.at[o - 1], grecv_x.at[o - 1], at_x(o)) for o in range(1, nx)]
    for copy in copies:
        copy.wait()
    mine = out_ref.at[rows(c * row_c, row_c)]
    send(mine, mine, gsend_c, grecv_c, at_c(1)).wait()


def reduce_all(part, nx, ny, nz):
    piece = part.shape[0] // (2 * nx * ny)
    vmem = pl.BlockSpec(memory_space=pltpu.VMEM)
    dma = pltpu.SemaphoreType.DMA
    def pair(count):
        return [dma((count,)), dma((count,))]
    return pl.pallas_call(
        functools.partial(reduce_kernel, nx, ny, nz, piece),
        out_shape=jax.ShapeDtypeStruct(part.shape, F32),
        in_specs=[vmem],
        out_specs=vmem,
        scratch_shapes=[
            pltpu.VMEM((piece * ny * nx, 128), F32),
            pltpu.VMEM((piece * ny, 128), F32),
            pltpu.VMEM((piece, 128), F32),
            pltpu.VMEM((piece * ny * nx, 128), F32),
            pltpu.VMEM((nx - 1, piece * ny, 128), F32),
            pltpu.VMEM((ny - 1, piece, 128), F32),
            pltpu.VMEM((nz, piece, 128), F32),
            dma, dma, *pair(nx - 1), *pair(ny - 1), *pair(nz - 1),
            dma, dma, *pair(nx - 1), *pair(ny - 1),
        ],
        name="reduce_all",
        compiler_params=pltpu.CompilerParams(collective_id=0, has_side_effects=True, vmem_limit_bytes=32 << 20),
    )(part)

TERMS=6; SG=16; PAN=32; LEVEL=0
def dot(a,b): return jnp.dot(a,b,preferred_element_type=F32)
def mm(a,b):
    if TERMS==3:
        ah,am=split(a,2); bh,bm=split(b,2)
        return dot(jnp.concatenate([ah,am],1),jnp.concatenate([bh,bh],0))+dot(ah,bm)
    if TERMS==1:
        return dot(a.astype(BF),b.astype(BF))
    return jnp.dot(a,b,precision=lax.Precision.HIGHEST,preferred_element_type=F32)

def bl(v,c): return jnp.broadcast_to(v[:,c:c+1],(8,128))
def bs(v,r): return jnp.broadcast_to(v[r:r+1,:],(8,128))

def invert(M):
    lane=lax.broadcasted_iota(jnp.int32,(8,128),1); sub=lax.broadcasted_iota(jnp.int32,(8,128),0)
    biglane=lax.broadcasted_iota(jnp.int32,(128,128),1)
    nq=PAN//8
    for p in range(128//PAN):
        p0=PAN*p
        S=[M[p0+8*q:p0+8*q+8,:] for q in range(nq)]
        for h in range(PAN//SG):
            B=[[bl(S[q],p0+SG*h+j) for q in range(nq)] for j in range(SG)]
            for j in range(SG):
                row=SG*h+j; qj,rj=divmod(row,8); c=p0+row
                inv=1.0/bs(B[j][qj],rj)
                here=lane==c; mine=sub==rj
                prow=jnp.where(here,1.0,bs(S[qj],rj))*inv
                for j2 in range(j+1,SG):
                    raw=bs(B[j2][qj],rj); bp=raw*inv
                    for q in range(nq):
                        u=B[j2][q]-((B[j][q]*raw)*inv if j2==j+1 else B[j][q]*bp)
                        B[j2][q]=jnp.where(mine,bp,u) if q==qj else u
                for q in range(nq):
                    u=jnp.where(here,0.0,S[q])-B[j][q]*prow
                    S[q]=jnp.where(mine,prow,u) if q==qj else u
        R=jnp.concatenate(S,axis=0)
        pad=[jnp.zeros((PAN,128),F32)]*(128//PAN); pad[p]=R
        Rp=jnp.concatenate(pad,axis=0)
        upd=jnp.where((biglane>=p0)&(biglane<p0+PAN),0.0,M)-mm(M,Rp)
        M=jnp.concatenate([x for x in [upd[:p0],R,upd[p0+PAN:]] if x.shape[0]],axis=0)
    return M

def eliminate(mat):
    for k in range(4):
        b=128*k
        Mi=invert(mat[b:b+128,b:b+128])
        R=mm(Mi,mat[b:b+128,b+128:])
        order=[(k+1+t)%4 for t in range(3)]
        if k<3:
            o=k+1
            mat[128*o:128*o+128,128*o:128*o+128]-=mm(mat[128*o:128*o+128,b:b+128],R[:,:128])
            mat[128*o:128*o+128,128*o+128:]-=mm(mat[128*o:128*o+128,b:b+128],R[:,128:])
            order=order[1:]
        for o in order:
            mat[128*o:128*o+128,b+128:]-=mm(mat[128*o:128*o+128,b:b+128],R)
        mat[b:b+128,b+128:]=R

def assemble(red_ref, mat, scale, root, ridge):
    r=lax.broadcasted_iota(jnp.int32,(128,128),0); c=lax.broadcasted_iota(jnp.int32,(128,128),1)
    for n,(i,j) in enumerate(PAIRS):
        b=red_ref[128*n:128*n+128,:]*scale
        if i==j: b=b+jnp.where(r==c,ridge,0.0)
        mat[128*i:128*i+128,128*j:128*j+128]=b
        if i!=j: mat[128*j:128*j+128,128*i:128*i+128]=b.T
    for i in range(4):
        row=red_ref[1280+i:1281+i,:]*root
        mat[128*i:128*i+128,512:640]=jnp.broadcast_to(row,(128,128)).T

def solve_kernel(scale, root, ridge, axis, red_ref, out_ref, mat):
    assemble(red_ref, mat, scale, root, ridge)
    if LEVEL!=1: eliminate(mat)
    me=lax.axis_index(axis) if axis else 1
    blk=mat[pl.ds(pl.multiple_of(me*128,128),128),512:640]
    out_ref[...]=blk.T[0:1,:]

def solve(red, scale, root, ridge, axis):
    return pl.pallas_call(functools.partial(solve_kernel,scale,root,ridge,axis),
        out_shape=jax.ShapeDtypeStruct((1,128),jnp.float32),
        in_specs=[pl.BlockSpec(memory_space=pltpu.VMEM)],out_specs=pl.BlockSpec(memory_space=pltpu.VMEM),
        scratch_shapes=[pltpu.VMEM((512,640),jnp.float32)],name="solve",
        compiler_params=pltpu.CompilerParams(vmem_limit_bytes=32<<20))(red)


def shards(mesh, pressure, mic_cycle, mic_azimuth, bin_index, source_cell):
    nx = mesh.shape["grp"]
    ny = 8
    nz = mesh.shape["row"] // (2 * ny)
    count = pressure.shape[1] * nx * mesh.shape["row"]
    part = panel(0.08, pressure, mic_cycle, mic_azimuth, bin_index, source_cell)
    total = reduce_all(part, nx, ny, nz)
    return solve(total, 1.0 / count, 1.0 / count**0.5, 0.5, "grp")


def solution(mesh):
    placed = (P(None, ("grp", "row")), P(None, ("grp", "row")), P(None, ("grp", "row")), P(), P())
    return jax.shard_map(
        functools.partial(shards, mesh), mesh=mesh, in_specs=placed, out_specs=P(None, "grp"), check_vma=False
    )
```

```python
import functools

import jax
import jax.numpy as jnp
import numpy as np
from jax import lax
from jax.experimental import pallas as pl
from jax.experimental.pallas import tpu as pltpu
from jax.sharding import PartitionSpec as P

F32 = jnp.float32
BF = jnp.bfloat16
S = 512
NRING = 4096
NAZ = 8192
PAIRS = [(i, j) for i in range(4) for j in range(i, 4)]

NT=(((1,),(1,)),((),()))
CHUNK=256
COS=[float(v) for v in (6.283185307179586,-41.34170224039975,81.60524927607504,-76.70585975306136,42.05869394489765)]
MAGIC=12582912.0

def split(v,n):
    parts=[]
    for _ in range(n-1):
        h=v.astype(BF); parts.append(h); v=v-h.astype(F32)
    parts.append(v.astype(BF)); return parts

def cos_turns(t, gain=None):
    y=t-((t+MAGIC)-MAGIC)
    v=0.25-jnp.abs(y)
    u=v*v
    s=COS[4]
    for c in COS[3::-1]: s=s*u+c
    return (s*v) if gain is None else s*(v*gain)

def panel_gram(loads, spacing, bin_ref, p_ref, cyc_ref, az_ref, src_ref, out_ref, src_scr, mic_scr, hi_scr, lo_scr):
    loads[0].wait()
    cell=src_ref[...].astype(F32)
    li=jnp.floor((cell+0.5)*0.01); rest=cell-100.0*li
    lj=jnp.floor((rest+0.5)*0.1); ll=rest-10.0*lj
    t=[2.0*v-9.0 for v in (li,lj,ll)]
    sq=t[0]*t[0]+t[1]*t[1]+t[2]*t[2]
    one=jnp.ones_like(sq); zero=jnp.zeros_like(sq)
    rows=[t[0]]*3+[t[1]]*3+[t[2]]*3+[sq]*3+[one]
    sT=jnp.concatenate(rows+[zero]*(128-len(rows)),axis=0)
    src_scr[...]=sT.T.astype(BF)
    loads[1].wait()
    loads[2].wait()
    half=spacing*0.5
    polar=(2*cyc_ref[...]+1).astype(F32)*(1.0/16384.0)
    azim=az_ref[...].astype(F32)*(1.0/8192.0)
    sp=cos_turns(polar-0.25); cp=cos_turns(polar)
    mic=[sp*cos_turns(azim), sp*cos_turns(azim-0.25), cp]
    mrows=[]
    for m in mic: mrows+=split(m*(-2.0*half),3)
    w=jnp.full(mic[0].shape,half*half,F32)
    mrows+=split(w,3)+[jnp.ones_like(w).astype(BF)]
    mrows=[m.astype(F32) for m in mrows]
    mrows+=[jnp.zeros_like(w)]*(16-len(mrows))
    mic_scr[...]=jnp.concatenate(mrows,axis=0).astype(BF)
    n=p_ref.shape[1]
    loads[3].wait()
    loads[4].wait()
    ph,pm=[v.astype(F32) for v in split(p_ref[...],2)]
    hi_scr[S:S+16,:]=jnp.concatenate([ph,pm]+[jnp.zeros_like(ph)]*14,axis=0).astype(BF)
    kc=1.5*(bin_ref[0].astype(F32)+1.0)*float(1/(2*np.pi))
    for c in range(n//CHUNK):
        cols=slice(c*CHUNK,(c+1)*CHUNK)
        d2=jnp.dot(src_scr[:,:16],mic_scr[:,cols],preferred_element_type=F32)
        r=lax.rsqrt(d2)
        val=cos_turns((d2*r)*kc, r)
        h=val.astype(BF)
        hi_scr[0:S,cols]=h
        lo_scr[:,cols]=(val-h.astype(F32)).astype(BF)
    H=lax.dot_general(hi_scr[...],hi_scr[0:S,:],NT,preferred_element_type=F32)
    L=lax.dot_general(hi_scr[...],lo_scr[...],NT,preferred_element_type=F32)
    nblk=0
    for i in range(4):
        for j in range(i,4):
            a=slice(128*i,128*i+128); b=slice(128*j,128*j+128)
            out_ref[128*nblk:128*nblk+128,:]=H[a,b]+L[a,b]+L[b,a].T
            nblk+=1
    r=(H[S:S+1]+L[S:S+1])+(H[S+1:S+2]+L[S+1:S+2])
    tail=jnp.concatenate([r[:,128*i:128*i+128] for i in range(4)]+[jnp.zeros((4,128),F32)],axis=0)
    out_ref[1280:1288,:]=tail
    out_ref[1288:1536,:]=jnp.zeros((248,128),F32)


MESH = pl.DeviceIdType.MESH
RING8 = (4, 3, 5, 2, 6, 1, 7)


def fit_kernel(dims, spacing, bin_hbm, p_hbm, cyc_hbm, az_hbm, src_hbm, out_ref,
               bin_ref, p_ref, cyc_ref, az_ref, src_ref, in_sem, src_scr, mic_scr, hi_scr, lo_scr,
               part, acc_c, acc_x, acc_y, buf_c, buf_x, buf_y, buf_z,
               send_c, recv_c, send_x, recv_x, send_y, recv_y, send_z, recv_z,
               gsend_c, grecv_c, gsend_x, grecv_x, gsend_y, grecv_y):
    nx, ny, nz, piece = dims
    x = lax.axis_index("grp")
    row = lax.axis_index("row")
    c = lax.rem(row, 2)
    y = lax.rem(row // 2, ny)
    z = row // (2 * ny)

    def at_c():
        return {"row": row + 1 - 2 * c}

    def at_x(o):
        return {"grp": lax.rem(x + o, nx)}

    def at_y(o):
        return {"row": row + 2 * (lax.rem(y + o, ny) - y)}

    def at_z(o):
        return {"row": row + 2 * ny * (lax.rem(z + o, nz) - z)}

    partners = [at_c()] + [at_x(o) for o in range(1, nx)] + [at_y(o) for o in range(1, ny)]
    partners += [at_z(o) for o in range(1, nz)]
    barrier = pltpu.get_barrier_semaphore()
    for partner in partners:
        pl.semaphore_signal(barrier, inc=1, device_id=partner, device_id_type=MESH)

    loads = []
    for n, (src, dst) in enumerate([(src_hbm, src_ref), (cyc_hbm, cyc_ref), (az_hbm, az_ref), (bin_hbm, bin_ref),
                                    (p_hbm, p_ref)]):
        load = pltpu.make_async_copy(src, dst, in_sem.at[n])
        load.start()
        loads.append(load)
    panel_gram(loads, spacing, bin_ref, p_ref, cyc_ref, az_ref, src_ref, part, src_scr, mic_scr, hi_scr, lo_scr)
    pl.semaphore_wait(barrier, len(partners))

    sends = []

    def send(src, dst, ssem, rsem, partner):
        copy = pltpu.make_async_remote_copy(src_ref=src, dst_ref=dst, send_sem=ssem, recv_sem=rsem,
                                            device_id=partner, device_id_type=MESH)
        copy.start()
        sends.append(copy)
        return copy

    def rows(start, count):
        return pl.ds(pl.multiple_of(start, 8), count)

    chunk = piece * nx

    def chunk_of(core, yy):
        return rows((core * ny + yy) * chunk, chunk)

    def piece_of(core, yy, xx):
        return rows(((core * ny + yy) * nx + xx) * piece, piece)

    far = [o for o in RING8 if o < ny] + [0]
    targets = [lax.rem(y + o, ny) for o in far]
    copies_c = [send(part.at[chunk_of(1 - c, t)], buf_c.at[i], send_c.at[i], recv_c.at[i], at_c())
                for i, t in enumerate(targets)]
    copies_x = []
    for i, t in enumerate(targets):
        copies_c[i].wait_recv()
        acc_c[i] = part[chunk_of(c, t), :] + buf_c[i]
        copies_x.append([
            send(acc_c.at[i, rows(lax.rem(x + o, nx) * piece, piece)], buf_x.at[i, o - 1],
                 send_x.at[i, o - 1], recv_x.at[i, o - 1], at_x(o)) for o in (2, 1, 3) if o < nx])
    copies_y = []
    for i, o in enumerate(far):
        for copy in copies_x[i]:
            copy.wait_recv()
        total = acc_c[i, rows(x * piece, piece), :]
        for k in range(nx - 1):
            total = total + buf_x[i, k]
        acc_x[i] = total
        if o:
            copies_y.append(send(acc_x.at[i], buf_y.at[o - 1], send_y.at[o - 1], recv_y.at[o - 1], at_y(o)))
    for copy in copies_y:
        copy.wait_recv()
    for k in range(ny - 1):
        total = total + buf_y[k]
    acc_y[...] = total
    copies_z = [send(acc_y, buf_z.at[z], send_z.at[o - 1], recv_z.at[o - 1], at_z(o)) for o in RING8 if o < nz]
    buf_z[z] = total
    for copy in copies_z:
        copy.wait_recv()
    total = buf_z[0]
    for k in range(1, nz):
        total = total + buf_z[k]
    mine = out_ref.at[piece_of(c, y, x)]
    mine[...] = total
    gather_y = {o: send(mine, mine, gsend_y.at[o - 1], grecv_y.at[o - 1], at_y(o)) for o in RING8 if o < ny}
    near = [0] + [o for o in RING8[::-1] if o < ny]
    sources = [lax.rem(y - o + ny, ny) for o in near]
    gather_x = []
    for i, o in enumerate(near):
        if o:
            gather_y[o].wait_recv()
        ref = out_ref.at[piece_of(c, sources[i], x)]
        gather_x.append([send(ref, ref, gsend_x.at[i, k - 1], grecv_x.at[i, k - 1], at_x(k))
                         for k in (2, 1, 3) if k < nx])
    gather_c = []
    for i in range(ny):
        for copy in gather_x[i]:
            copy.wait_recv()
        ref = out_ref.at[chunk_of(c, sources[i])]
        gather_c.append(send(ref, ref, gsend_c.at[i], grecv_c.at[i], at_c()))
    for copy in gather_c:
        copy.wait_recv()
    for copy in sends:
        copy.wait_send()


def fit(spacing, nx, ny, nz, p, cyc, az, b, src):
    n = p.shape[1]
    rows = 1536
    piece = rows // (2 * nx * ny)
    anywhere = pl.BlockSpec(memory_space=pltpu.HBM)
    dma = pltpu.SemaphoreType.DMA
    v = pltpu.VMEM

    def pair(*shape):
        return [dma(shape), dma(shape)]

    return pl.pallas_call(
        functools.partial(fit_kernel, (nx, ny, nz, piece), spacing),
        out_shape=jax.ShapeDtypeStruct((rows, 128), F32),
        in_specs=[anywhere] * 5,
        out_specs=pl.BlockSpec(memory_space=pltpu.VMEM),
        scratch_shapes=[
            pltpu.SMEM((1,), jnp.int32), v((1, n), F32), v((1, n), jnp.int32), v((1, n), jnp.int32),
            v((1, S), jnp.int32), dma((5,)),
            v((S, 128), BF), v((16, n), BF), v((S + 16, n), BF), v((S, n), BF),
            v((rows, 128), F32),
            v((ny, piece * nx, 128), F32), v((ny, piece, 128), F32), v((piece, 128), F32),
            v((ny, piece * nx, 128), F32), v((ny, nx - 1, piece, 128), F32), v((ny - 1, piece, 128), F32),
            v((nz, piece, 128), F32),
            *pair(ny), *pair(ny, nx - 1), *pair(ny - 1), *pair(nz - 1),
            *pair(ny), *pair(ny, nx - 1), *pair(ny - 1),
        ],
        name="fit",
        compiler_params=pltpu.CompilerParams(collective_id=0, has_side_effects=True, vmem_limit_bytes=40 << 20),
    )(b, p, cyc, az, src.reshape(1, S))

TERMS=6; SG=16; PAN=32; LEVEL=0
def dot(a,b): return jnp.dot(a,b,preferred_element_type=F32)
def mm(a,b):
    if TERMS==3:
        ah,am=split(a,2); bh,bm=split(b,2)
        return dot(jnp.concatenate([ah,am],1),jnp.concatenate([bh,bh],0))+dot(ah,bm)
    if TERMS==1:
        return dot(a.astype(BF),b.astype(BF))
    return jnp.dot(a,b,precision=lax.Precision.HIGHEST,preferred_element_type=F32)

def bl(v,c): return jnp.broadcast_to(v[:,c:c+1],(8,128))
def bs(v,r): return jnp.broadcast_to(v[r:r+1,:],(8,128))

def invert(M):
    lane=lax.broadcasted_iota(jnp.int32,(8,128),1); sub=lax.broadcasted_iota(jnp.int32,(8,128),0)
    biglane=lax.broadcasted_iota(jnp.int32,(128,128),1)
    nq=PAN//8
    for p in range(128//PAN):
        p0=PAN*p
        S=[M[p0+8*q:p0+8*q+8,:] for q in range(nq)]
        for h in range(PAN//SG):
            B=[jnp.stack([jnp.broadcast_to(S[q][:,c:c+1],(8,128)) for c in range(p0+SG*h,p0+SG*h+SG)]) for q in range(nq)]
            for j in range(SG):
                row=SG*h+j; qj,rj=divmod(row,8); c=p0+row
                here=lane==c; mine=sub==rj
                inv=1.0/B[qj][0,rj:rj+1,:]
                prow=jnp.where(here[:1],1.0,S[qj][rj:rj+1,:])*inv
                col=[B[q][0] for q in range(nq)]
                if j<SG-1:
                    raw=B[qj][1:,rj:rj+1,:]
                    bp=raw*inv
                    for q in range(nq):
                        nxt=B[q][1:]-col[q]*bp
                        B[q]=jnp.where(mine,bp,nxt) if q==qj else nxt
                for q in range(nq):
                    u=jnp.where(here,0.0,S[q])-col[q]*prow
                    S[q]=jnp.where(mine,prow,u) if q==qj else u
        R=jnp.concatenate(S,axis=0)
        pad=[jnp.zeros((PAN,128),F32)]*(128//PAN); pad[p]=R
        Rp=jnp.concatenate(pad,axis=0)
        upd=jnp.where((biglane>=p0)&(biglane<p0+PAN),0.0,M)-mm(M,Rp)
        M=jnp.concatenate([x for x in [upd[:p0],R,upd[p0+PAN:]] if x.shape[0]],axis=0)
    return M

def eliminate(mat):
    if LEVEL==2:
        M=mat[0:128,0:128]
        for k in range(4): M=invert(M)
        mat[0:128,0:128]=M
        return
    for k in range(4):
        b=128*k
        Mi=invert(mat[b:b+128,b:b+128])
        R=mm(Mi,mat[b:b+128,b+128:])
        order=[(k+1+t)%4 for t in range(3)]
        if k<3:
            o=k+1
            mat[128*o:128*o+128,128*o:128*o+128]-=mm(mat[128*o:128*o+128,b:b+128],R[:,:128])
            mat[128*o:128*o+128,128*o+128:]-=mm(mat[128*o:128*o+128,b:b+128],R[:,128:])
            order=order[1:]
        for o in order:
            mat[128*o:128*o+128,b+128:]-=mm(mat[128*o:128*o+128,b:b+128],R)
        mat[b:b+128,b+128:]=R

def assemble(red_ref, mat, scale, root, ridge):
    r=lax.broadcasted_iota(jnp.int32,(128,128),0); c=lax.broadcasted_iota(jnp.int32,(128,128),1)
    for n,(i,j) in enumerate(PAIRS):
        b=red_ref[128*n:128*n+128,:]*scale
        if i==j: b=b+jnp.where(r==c,ridge,0.0)
        mat[128*i:128*i+128,128*j:128*j+128]=b
        if i!=j: mat[128*j:128*j+128,128*i:128*i+128]=b.T
    for i in range(4):
        row=red_ref[1280+i:1281+i,:]*root
        mat[128*i:128*i+128,512:640]=jnp.broadcast_to(row,(128,128)).T

def solve_kernel(scale, root, ridge, axis, red_ref, out_ref, mat):
    assemble(red_ref, mat, scale, root, ridge)
    if LEVEL!=1: eliminate(mat)
    me=lax.axis_index(axis) if axis else 1
    blk=mat[pl.ds(pl.multiple_of(me*128,128),128),512:640]
    out_ref[...]=blk.T[0:1,:]

def solve(red, scale, root, ridge, axis):
    return pl.pallas_call(functools.partial(solve_kernel,scale,root,ridge,axis),
        out_shape=jax.ShapeDtypeStruct((1,128),jnp.float32),
        in_specs=[pl.BlockSpec(memory_space=pltpu.VMEM)],out_specs=pl.BlockSpec(memory_space=pltpu.VMEM),
        scratch_shapes=[pltpu.VMEM((512,640),jnp.float32)],name="solve",
        compiler_params=pltpu.CompilerParams(vmem_limit_bytes=32<<20))(red)


def shards(mesh, pressure, mic_cycle, mic_azimuth, bin_index, source_cell):
    nx = mesh.shape["grp"]
    ny = 8
    nz = mesh.shape["row"] // (2 * ny)
    count = pressure.shape[1] * nx * mesh.shape["row"]
    total = fit(0.08, nx, ny, nz, pressure, mic_cycle, mic_azimuth, bin_index, source_cell)
    return solve(total, 1.0 / count, 1.0 / count**0.5, 0.5, "grp")


def solution(mesh):
    placed = (P(None, ("grp", "row")), P(None, ("grp", "row")), P(None, ("grp", "row")), P(), P())
    return jax.shard_map(
        functools.partial(shards, mesh), mesh=mesh, in_specs=placed, out_specs=P(None, "grp"), check_vma=False
    )
```

```python
import functools

import jax
import jax.numpy as jnp
import numpy as np
from jax import lax
from jax.experimental import pallas as pl
from jax.experimental.pallas import tpu as pltpu
from jax.sharding import PartitionSpec as P

F32 = jnp.float32
BF = jnp.bfloat16
S = 512
NRING = 4096
NAZ = 8192
PAIRS = [(i, j) for i in range(4) for j in range(i, 4)]

NT=(((1,),(1,)),((),()))
CHUNK=256
SINE=(6.283185160089467, -41.341655031414675, 81.60100407316348, -76.54978229140988, 39.5367060495799)
MAGIC=12582912.0

def split(v,n):
    parts=[]
    for _ in range(n-1):
        h=v.astype(BF); parts.append(h); v=v-h.astype(F32)
    parts.append(v.astype(BF)); return parts

def cos_turns(t, gain=None):
    y=t-((t+MAGIC)-MAGIC)
    v=0.25-jnp.abs(y)
    u=v*v
    s=SINE[4]
    for c in SINE[3::-1]: s=s*u+c
    return (s*v) if gain is None else s*(v*gain)

def panel_gram(loads, spacing, bin_ref, p_ref, cyc_ref, az_ref, src_ref, out_ref, src_scr, mic_scr, hi_scr, lo_scr):
    loads[0].wait()
    cell=src_ref[...].astype(F32)
    li=jnp.floor((cell+0.5)*0.01); rest=cell-100.0*li
    lj=jnp.floor((rest+0.5)*0.1); ll=rest-10.0*lj
    t=[2.0*v-9.0 for v in (li,lj,ll)]
    sq=t[0]*t[0]+t[1]*t[1]+t[2]*t[2]
    one=jnp.ones_like(sq); zero=jnp.zeros_like(sq)
    rows=[t[0]]*3+[t[1]]*3+[t[2]]*3+[sq]*3+[one]
    sT=jnp.concatenate(rows+[zero]*(128-len(rows)),axis=0)
    src_scr[...]=sT.T.astype(BF)
    loads[1].wait()
    loads[2].wait()
    half=spacing*0.5
    polar=(2*cyc_ref[...]+1).astype(F32)*(1.0/16384.0)
    azim=az_ref[...].astype(F32)*(1.0/8192.0)
    sp=cos_turns(polar-0.25); cp=cos_turns(polar)
    mic=[sp*cos_turns(azim), sp*cos_turns(azim-0.25), cp]
    mrows=[]
    for m in mic: mrows+=split(m*(-2.0*half),3)
    w=jnp.full(mic[0].shape,half*half,F32)
    mrows+=split(w,3)+[jnp.ones_like(w).astype(BF)]
    mrows=[m.astype(F32) for m in mrows]
    mrows+=[jnp.zeros_like(w)]*(16-len(mrows))
    mic_scr[...]=jnp.concatenate(mrows,axis=0).astype(BF)
    n=p_ref.shape[1]
    loads[3].wait()
    loads[4].wait()
    ph,pm=[v.astype(F32) for v in split(p_ref[...],2)]
    hi_scr[S:S+16,:]=jnp.concatenate([ph,pm]+[jnp.zeros_like(ph)]*14,axis=0).astype(BF)
    kc=1.5*(bin_ref[0].astype(F32)+1.0)*float(1/(2*np.pi))
    for c in range(n//CHUNK):
        cols=slice(c*CHUNK,(c+1)*CHUNK)
        d2=jnp.dot(src_scr[:,:16],mic_scr[:,cols],preferred_element_type=F32)
        r=lax.rsqrt(d2)
        val=cos_turns((d2*r)*kc, r)
        h=val.astype(BF)
        hi_scr[0:S,cols]=h
        lo_scr[:,cols]=(val-h.astype(F32)).astype(BF)
    H=lax.dot_general(hi_scr[...],hi_scr[0:S,:],NT,preferred_element_type=F32)
    L=lax.dot_general(hi_scr[...],lo_scr[...],NT,preferred_element_type=F32)
    nblk=0
    for i in range(4):
        for j in range(i,4):
            a=slice(128*i,128*i+128); b=slice(128*j,128*j+128)
            out_ref[128*nblk:128*nblk+128,:]=H[a,b]+L[a,b]+L[b,a].T
            nblk+=1
    r=(H[S:S+1]+L[S:S+1])+(H[S+1:S+2]+L[S+1:S+2])
    tail=jnp.concatenate([r[:,128*i:128*i+128] for i in range(4)]+[jnp.zeros((4,128),F32)],axis=0)
    out_ref[1280:1288,:]=tail
    out_ref[1288:1536,:]=jnp.zeros((248,128),F32)


TERMS=6; INNER=3; SG=16
def dot(a,b): return jnp.dot(a,b,preferred_element_type=F32)
def mm(a,b):
    if TERMS==3:
        ah,am=split(a,2); bh,bm=split(b,2)
        return dot(jnp.concatenate([ah,am],1),jnp.concatenate([bh,bh],0))+dot(ah,bm)
    if TERMS==6:
        ah,am,al=split(a,3); bh,bm,bl_=split(b,3)
        ahm=jnp.concatenate([ah,am],1)
        return (dot(jnp.concatenate([ah,al],1),jnp.concatenate([bl_,bh],0))+dot(ahm,jnp.concatenate([bm,bm],0)))+dot(ahm,jnp.concatenate([bh,bh],0))
    if TERMS==1:
        return dot(a.astype(BF),b.astype(BF))
    return jnp.dot(a,b,precision=lax.Precision.HIGHEST,preferred_element_type=F32)

def bl(v,c): return jnp.broadcast_to(v[:,c:c+1],(8,128))
def bs(v,r): return jnp.broadcast_to(v[r:r+1,:],(8,128))

def mm_inner(a,b):
    if INNER==3:
        ah,am=split(a,2); bh,bm=split(b,2)
        return dot(jnp.concatenate([ah,am],1),jnp.concatenate([bh,bh],0))+dot(ah,bm)
    if INNER==6:
        ah,am,al=split(a,3); bh,bm,bl_=split(b,3)
        ahm=jnp.concatenate([ah,am],1)
        return (dot(jnp.concatenate([ah,al],1),jnp.concatenate([bl_,bh],0))+dot(ahm,jnp.concatenate([bm,bm],0)))+dot(ahm,jnp.concatenate([bh,bh],0))
    return jnp.dot(a,b,precision=lax.Precision.HIGHEST,preferred_element_type=F32)

def sweep(S, first, c0, lane, sub):
    nq=len(S)
    B=[jnp.stack([jnp.broadcast_to(S[q][:,c:c+1],(8,128)) for c in range(c0,c0+SG)]) for q in range(nq)]
    piv=(lane>=c0)&(lane<c0+SG)
    for q in range(nq):
        fill=jnp.where(lane-c0==sub+(8*q-first),1.0,0.0) if first<=8*q<first+SG else 0.0
        S[q]=jnp.where(piv,fill,S[q])
    scale=[None]*nq
    for j in range(SG):
        qj,rj=divmod(first+j,8)
        mine=sub==rj
        inv=1.0/jnp.broadcast_to(B[qj][0,rj:rj+1,:],(8,128))
        rawS=S[qj][rj:rj+1,:]
        g=[(jnp.where(mine,0.0,B[q][0]) if q==qj else B[q][0])*inv for q in range(nq)]
        scale[qj]=inv if scale[qj] is None else jnp.where(sub>=rj,inv,scale[qj])
        if j<SG-1:
            raw=B[qj][1:,rj:rj+1,:]
            B=[B[q][1:]-g[q]*raw for q in range(nq)]
        S=[S[q]-g[q]*rawS for q in range(nq)]
    return [S[q] if scale[q] is None else S[q]*scale[q] for q in range(nq)]

def invert(M):
    lane=lax.broadcasted_iota(jnp.int32,(8,128),1); sub=lax.broadcasted_iota(jnp.int32,(8,128),0)
    biglane=lax.broadcasted_iota(jnp.int32,(128,128),1)
    def put(rows, start, into):
        return jnp.concatenate([x for x in [into[:start],rows,into[start+rows.shape[0]:]] if x.shape[0]],axis=0)
    zero=jnp.zeros((128,128),F32)
    ahead=[M[8*q:8*q+8,:] for q in range(2)]
    for g in range(8):
        p0=16*g
        S=ahead+([M[p0+16+8*q:p0+24+8*q,:] for q in range(2)] if g<7 else [])
        S=sweep(S,0,p0,lane,sub)
        ahead=S[2:]
        R=jnp.concatenate(S[:2],axis=0)
        M=jnp.where((biglane>=p0)&(biglane<p0+16),0.0,M)-mm_inner(M,put(R,p0,zero))
        M=put(R,p0,M)
    return M

def eliminate(mat):
    for k in range(4):
        b=128*k
        Mi=invert(mat[b:b+128,b:b+128])
        R=mm(Mi,mat[b:b+128,b+128:])
        order=[(k+1+t)%4 for t in range(3)]
        if k<3:
            o=k+1
            mat[128*o:128*o+128,128*o:128*o+128]-=mm(mat[128*o:128*o+128,b:b+128],R[:,:128])
            mat[128*o:128*o+128,128*o+128:]-=mm(mat[128*o:128*o+128,b:b+128],R[:,128:])
            order=order[1:]
        for o in order:
            mat[128*o:128*o+128,b+128:]-=mm(mat[128*o:128*o+128,b:b+128],R)
        mat[b:b+128,b+128:]=R

def assemble(red_ref, mat, scale, root, ridge):
    r=lax.broadcasted_iota(jnp.int32,(128,128),0); c=lax.broadcasted_iota(jnp.int32,(128,128),1)
    for n,(i,j) in enumerate(PAIRS):
        b=red_ref[128*n:128*n+128,:]*scale
        if i==j: b=b+jnp.where(r==c,ridge,0.0)
        mat[128*i:128*i+128,128*j:128*j+128]=b
        if i!=j: mat[128*j:128*j+128,128*i:128*i+128]=b.T
    for i in range(4):
        row=red_ref[1280+i:1281+i,:]*root
        mat[128*i:128*i+128,512:640]=jnp.broadcast_to(row,(128,128)).T


MESH = pl.DeviceIdType.MESH
RING8 = (4, 3, 5, 2, 6, 1, 7)


def fit_kernel(dims, consts, bin_hbm, p_hbm, cyc_hbm, az_hbm, src_hbm, out_ref,
               bin_ref, p_ref, cyc_ref, az_ref, src_ref, in_sem, src_scr, mic_scr, hi_scr, lo_scr,
               part, full, mat, acc_c, acc_x, acc_y, buf_c, buf_x, buf_y, buf_z,
               send_c, recv_c, send_x, recv_x, send_y, recv_y, send_z, recv_z,
               gsend_c, grecv_c, gsend_x, grecv_x, gsend_y, grecv_y):
    nx, ny, nz, piece = dims
    x = lax.axis_index("grp")
    row = lax.axis_index("row")
    c = lax.rem(row, 2)
    y = lax.rem(row // 2, ny)
    z = row // (2 * ny)

    def at_c():
        return {"row": row + 1 - 2 * c}

    def at_x(o):
        return {"grp": lax.rem(x + o, nx)}

    def at_y(o):
        return {"row": row + 2 * (lax.rem(y + o, ny) - y)}

    def at_z(o):
        return {"row": row + 2 * ny * (lax.rem(z + o, nz) - z)}

    partners = [at_c()] + [at_x(o) for o in range(1, nx)] + [at_y(o) for o in range(1, ny)]
    partners += [at_z(o) for o in range(1, nz)]
    barrier = pltpu.get_barrier_semaphore()
    for partner in partners:
        pl.semaphore_signal(barrier, inc=1, device_id=partner, device_id_type=MESH)

    loads = []
    for n, (src, dst) in enumerate([(src_hbm, src_ref), (cyc_hbm, cyc_ref), (az_hbm, az_ref), (bin_hbm, bin_ref),
                                    (p_hbm, p_ref)]):
        load = pltpu.make_async_copy(src, dst, in_sem.at[n])
        load.start()
        loads.append(load)
    scale, root, ridge, spacing = consts
    panel_gram(loads, spacing, bin_ref, p_ref, cyc_ref, az_ref, src_ref, part, src_scr, mic_scr, hi_scr, lo_scr)
    pl.semaphore_wait(barrier, len(partners))

    sends = []

    def send(src, dst, ssem, rsem, partner):
        copy = pltpu.make_async_remote_copy(src_ref=src, dst_ref=dst, send_sem=ssem, recv_sem=rsem,
                                            device_id=partner, device_id_type=MESH)
        copy.start()
        sends.append(copy)
        return copy

    def rows(start, count):
        return pl.ds(pl.multiple_of(start, 8), count)

    chunk = piece * nx

    def chunk_of(core, yy):
        return rows((core * ny + yy) * chunk, chunk)

    def piece_of(core, yy, xx):
        return rows(((core * ny + yy) * nx + xx) * piece, piece)

    far = [o for o in RING8 if o < ny] + [0]
    targets = [lax.rem(y + o, ny) for o in far]
    copies_c = [send(part.at[chunk_of(1 - c, t)], buf_c.at[i], send_c.at[i], recv_c.at[i], at_c())
                for i, t in enumerate(targets)]
    copies_x = []
    for i, t in enumerate(targets):
        copies_c[i].wait_recv()
        acc_c[i] = part[chunk_of(c, t), :] + buf_c[i]
        copies_x.append([
            send(acc_c.at[i, rows(lax.rem(x + o, nx) * piece, piece)], buf_x.at[i, o - 1],
                 send_x.at[i, o - 1], recv_x.at[i, o - 1], at_x(o)) for o in (2, 1, 3) if o < nx])
    copies_y = []
    for i, o in enumerate(far):
        for copy in copies_x[i]:
            copy.wait_recv()
        total = acc_c[i, rows(x * piece, piece), :]
        for k in range(nx - 1):
            total = total + buf_x[i, k]
        acc_x[i] = total
        if o:
            copies_y.append(send(acc_x.at[i], buf_y.at[o - 1], send_y.at[o - 1], recv_y.at[o - 1], at_y(o)))
    for copy in copies_y:
        copy.wait_recv()
    for k in range(ny - 1):
        total = total + buf_y[k]
    acc_y[...] = total
    copies_z = [send(acc_y, buf_z.at[z], send_z.at[o - 1], recv_z.at[o - 1], at_z(o)) for o in RING8 if o < nz]
    buf_z[z] = total
    for copy in copies_z:
        copy.wait_recv()
    total = buf_z[0]
    for k in range(1, nz):
        total = total + buf_z[k]
    mine = full.at[piece_of(c, y, x)]
    mine[...] = total
    gather_y = {o: send(mine, mine, gsend_y.at[o - 1], grecv_y.at[o - 1], at_y(o)) for o in RING8 if o < ny}
    near = [0] + [o for o in RING8[::-1] if o < ny]
    sources = [lax.rem(y - o + ny, ny) for o in near]
    gather_x = []
    for i, o in enumerate(near):
        if o:
            gather_y[o].wait_recv()
        ref = full.at[piece_of(c, sources[i], x)]
        gather_x.append([send(ref, ref, gsend_x.at[i, k - 1], grecv_x.at[i, k - 1], at_x(k))
                         for k in (2, 1, 3) if k < nx])
    gather_c = []
    for i in range(ny):
        for copy in gather_x[i]:
            copy.wait_recv()
        ref = full.at[chunk_of(c, sources[i])]
        gather_c.append(send(ref, ref, gsend_c.at[i], grecv_c.at[i], at_c()))
    for copy in gather_c:
        copy.wait_recv()
    assemble(full, mat, scale, root, ridge)
    eliminate(mat)
    block = mat[pl.ds(pl.multiple_of(x * 128, 128), 128), 512:640]
    out_ref[...] = block.T[0:1, :]
    for copy in sends:
        copy.wait_send()


def fit(consts, nx, ny, nz, p, cyc, az, b, src):
    n = p.shape[1]
    rows = 1536
    piece = rows // (2 * nx * ny)
    anywhere = pl.BlockSpec(memory_space=pl.ANY)
    dma = pltpu.SemaphoreType.DMA
    v = pltpu.VMEM

    def pair(*shape):
        return [dma(shape), dma(shape)]

    return pl.pallas_call(
        functools.partial(fit_kernel, (nx, ny, nz, piece), consts),
        out_shape=jax.ShapeDtypeStruct((1, 128), F32),
        in_specs=[anywhere] * 5,
        out_specs=pl.BlockSpec(memory_space=pltpu.VMEM),
        scratch_shapes=[
            pltpu.SMEM((1,), jnp.int32), v((1, n), F32), v((1, n), jnp.int32), v((1, n), jnp.int32),
            v((1, S), jnp.int32), dma((5,)),
            v((S, 128), BF), v((16, n), BF), v((S + 16, n), BF), v((S, n), BF),
            v((rows, 128), F32), v((rows, 128), F32), v((512, 640), F32),
            v((ny, piece * nx, 128), F32), v((ny, piece, 128), F32), v((piece, 128), F32),
            v((ny, piece * nx, 128), F32), v((ny, nx - 1, piece, 128), F32), v((ny - 1, piece, 128), F32),
            v((nz, piece, 128), F32),
            *pair(ny), *pair(ny, nx - 1), *pair(ny - 1), *pair(nz - 1),
            *pair(ny), *pair(ny, nx - 1), *pair(ny - 1),
        ],
        name="fit",
        compiler_params=pltpu.CompilerParams(collective_id=0, has_side_effects=True, vmem_limit_bytes=56 << 20),
    )(b, p, cyc, az, src.reshape(1, S))


def shards(mesh, pressure, mic_cycle, mic_azimuth, bin_index, source_cell):
    nx = mesh.shape["grp"]
    ny = 8
    nz = mesh.shape["row"] // (2 * ny)
    count = pressure.shape[1] * nx * mesh.shape["row"]
    consts = (1.0 / count, 1.0 / count**0.5, 0.5, 0.08)
    return fit(consts, nx, ny, nz, pressure, mic_cycle, mic_azimuth, bin_index, source_cell)


def solution(mesh):
    placed = (P(None, ("grp", "row")), P(None, ("grp", "row")), P(None, ("grp", "row")), P(), P())
    return jax.shard_map(
        functools.partial(shards, mesh), mesh=mesh, in_specs=placed, out_specs=P(None, "grp"), check_vma=False
    )
```

```python
import functools

import jax
import jax.numpy as jnp
import numpy as np
from jax import lax
from jax.experimental import pallas as pl
from jax.experimental.pallas import tpu as pltpu
from jax.sharding import PartitionSpec as P

F32 = jnp.float32
BF = jnp.bfloat16
S = 512
NRING = 4096
NAZ = 8192
PAIRS = [(i, j) for i in range(4) for j in range(i, 4)]

NT=(((1,),(1,)),((),()))
CHUNK=512
SINE=(6.283185160089467, -41.341655031414675, 81.60100407316348, -76.54978229140988, 39.5367060495799)
MAGIC=12582912.0

def split(v,n):
    parts=[]
    for _ in range(n-1):
        h=v.astype(BF); parts.append(h); v=v-h.astype(F32)
    parts.append(v.astype(BF)); return parts

def cos_turns(t, gain=None):
    y=t-((t+MAGIC)-MAGIC)
    v=0.25-jnp.abs(y)
    u=v*v
    s=SINE[4]
    for c in SINE[3::-1]: s=s*u+c
    return (s*v) if gain is None else s*(v*gain)

def bf16_parts(value, n):
    parts = []
    for _ in range(n):
        part = float(np.float32(value).astype(jnp.bfloat16))
        parts.append(part)
        value -= part
    return parts


UNIT=bf16_parts((1.5/(2*np.pi))**2, 3)
HALF=256


def order_of(bin_ref):
    order = bin_ref[0].astype(F32) + 1.0
    return order * order


def panel_gram(loads, spacing, bin_ref, p_ref, cyc_ref, az_ref, src_ref, out_ref, src_scr, mic_scr, hi_scr, lo_scr):
    loads[0].wait()
    loads[3].wait()
    cell=src_ref[...].astype(F32)
    li=jnp.floor((cell+0.5)*0.01); rest=cell-100.0*li
    lj=jnp.floor((rest+0.5)*0.1); ll=rest-10.0*lj
    t=[2.0*v-9.0 for v in (li,lj,ll)]
    sq=t[0]*t[0]+t[1]*t[1]+t[2]*t[2]
    one=jnp.ones_like(sq); zero=jnp.zeros_like(sq)
    sq_order=one*(order_of(bin_ref))
    rows=[t[0]]*3+[t[1]]*3+[t[2]]*3+[sq]*3+[sq_order]*3
    sT=jnp.concatenate(rows+[zero]*(128-len(rows)),axis=0)
    src_scr[...]=sT.T.astype(BF)
    loads[1].wait()
    loads[2].wait()
    order=bin_ref[0].astype(F32)+1.0
    turns=(order*order)*float((1.5/(2*np.pi))**2)
    half=spacing*0.5
    polar=(2*cyc_ref[...]+1).astype(F32)*(1.0/16384.0)
    azim=az_ref[...].astype(F32)*(1.0/8192.0)
    sp=cos_turns(polar-0.25); cp=cos_turns(polar)
    mic=[sp*cos_turns(azim), sp*cos_turns(azim-0.25), cp]
    mrows=[]
    for m in mic: mrows+=split(m*(turns*(-2.0*half)),3)
    w=jnp.full(mic[0].shape,half*half,F32)*turns
    mrows+=split(w,3)+[jnp.full(w.shape,v,BF) for v in UNIT]
    mrows=[m.astype(F32) for m in mrows]
    mrows+=[jnp.zeros_like(w)]*(16-len(mrows))
    mic_scr[...]=jnp.concatenate(mrows,axis=0).astype(BF)
    n=p_ref.shape[1]
    loads[4].wait()
    ph,pm=[v.astype(F32) for v in split(p_ref[...],2)]
    hi_scr[HALF:HALF+16,:]=jnp.concatenate([ph,pm]+[jnp.zeros_like(ph)]*14,axis=0).astype(BF)
    for lo in range(0, S, HALF):
        for c in range(n//CHUNK):
            cols=slice(c*CHUNK,(c+1)*CHUNK)
            t2=jnp.dot(src_scr[lo:lo+HALF,:16],mic_scr[:,cols],preferred_element_type=F32)
            r=lax.rsqrt(t2)
            val=cos_turns(t2*r, r)
            h=val.astype(BF)
            hi_scr[lo+(16 if lo else 0):lo+(16 if lo else 0)+HALF,cols]=h
            lo_scr[lo:lo+HALF,cols]=(val-h.astype(F32)).astype(BF)
    unit=1.5*(bin_ref[0].astype(F32)+1.0)*float(1/(2*np.pi))
    gain=unit*unit
    def product(a, b):
        return lax.dot_general(a, b, NT, preferred_element_type=F32)
    R0=HALF+16
    H1=product(hi_scr[0:R0],hi_scr[0:HALF]); L1=product(hi_scr[...],lo_scr[0:HALF])
    H2=product(hi_scr[...],hi_scr[R0:]); L2=product(hi_scr[...],lo_scr[HALF:S])
    def at(i):
        return 128*i+(16 if i>=2 else 0)
    def hblk(i,j):
        m=H1 if j<2 else H2
        return m[at(i):at(i)+128,128*(j%2):128*(j%2)+128]
    def lblk(i,j):
        m=L1 if j<2 else L2
        return m[at(i):at(i)+128,128*(j%2):128*(j%2)+128]
    for k,(i,j) in enumerate(PAIRS):
        out_ref[128*k:128*k+128,:]=((hblk(i,j)+lblk(i,j))+lblk(j,i).T)*gain
    r1=(H1[HALF:HALF+1]+L1[HALF:HALF+1])+(H1[HALF+1:HALF+2]+L1[HALF+1:HALF+2])
    r2=(H2[HALF:HALF+1]+L2[HALF:HALF+1])+(H2[HALF+1:HALF+2]+L2[HALF+1:HALF+2])
    tail=jnp.concatenate([r1[:,:128],r1[:,128:],r2[:,:128],r2[:,128:],jnp.zeros((4,128),F32)],axis=0)
    out_ref[1280:1288,:]=tail*unit
    out_ref[1288:1536,:]=jnp.zeros((248,128),F32)

TERMS=6; INNER=3; SG=16
def dot(a,b): return jnp.dot(a,b,preferred_element_type=F32)
def mm(a,b):
    if TERMS==3:
        ah,am=split(a,2); bh,bm=split(b,2)
        return dot(jnp.concatenate([ah,am],1),jnp.concatenate([bh,bh],0))+dot(ah,bm)
    if TERMS==6:
        ah,am,al=split(a,3); bh,bm,bl_=split(b,3)
        ahm=jnp.concatenate([ah,am],1)
        return (dot(jnp.concatenate([ah,al],1),jnp.concatenate([bl_,bh],0))+dot(ahm,jnp.concatenate([bm,bm],0)))+dot(ahm,jnp.concatenate([bh,bh],0))
    if TERMS==1:
        return dot(a.astype(BF),b.astype(BF))
    return jnp.dot(a,b,precision=lax.Precision.HIGHEST,preferred_element_type=F32)

def bl(v,c): return jnp.broadcast_to(v[:,c:c+1],(8,128))
def bs(v,r): return jnp.broadcast_to(v[r:r+1,:],(8,128))

def mm_inner(a,b):
    if INNER==3:
        ah,am=split(a,2); bh,bm=split(b,2)
        return dot(jnp.concatenate([ah,am],1),jnp.concatenate([bh,bh],0))+dot(ah,bm)
    if INNER==6:
        ah,am,al=split(a,3); bh,bm,bl_=split(b,3)
        ahm=jnp.concatenate([ah,am],1)
        return (dot(jnp.concatenate([ah,al],1),jnp.concatenate([bl_,bh],0))+dot(ahm,jnp.concatenate([bm,bm],0)))+dot(ahm,jnp.concatenate([bh,bh],0))
    return jnp.dot(a,b,precision=lax.Precision.HIGHEST,preferred_element_type=F32)

def sweep(S, first, c0, lane, sub):
    nq=len(S)
    B=[jnp.stack([jnp.broadcast_to(S[q][:,c:c+1],(8,128)) for c in range(c0,c0+SG)]) for q in range(nq)]
    piv=(lane>=c0)&(lane<c0+SG)
    for q in range(nq):
        fill=jnp.where(lane-c0==sub+(8*q-first),1.0,0.0) if first<=8*q<first+SG else 0.0
        S[q]=jnp.where(piv,fill,S[q])
    scale=[None]*nq
    for j in range(SG):
        qj,rj=divmod(first+j,8)
        mine=sub==rj
        inv=1.0/jnp.broadcast_to(B[qj][0,rj:rj+1,:],(8,128))
        rawS=S[qj][rj:rj+1,:]
        g=[(jnp.where(mine,0.0,B[q][0]) if q==qj else B[q][0])*inv for q in range(nq)]
        scale[qj]=inv if scale[qj] is None else jnp.where(sub>=rj,inv,scale[qj])
        if j<SG-1:
            raw=B[qj][1:,rj:rj+1,:]
            B=[B[q][1:]-g[q]*raw for q in range(nq)]
        S=[S[q]-g[q]*rawS for q in range(nq)]
    return [S[q] if scale[q] is None else S[q]*scale[q] for q in range(nq)]

def invert(M, between=None):
    lane=lax.broadcasted_iota(jnp.int32,(8,128),1); sub=lax.broadcasted_iota(jnp.int32,(8,128),0)
    biglane=lax.broadcasted_iota(jnp.int32,(128,128),1)
    def put(rows, start, into):
        return jnp.concatenate([x for x in [into[:start],rows,into[start+rows.shape[0]:]] if x.shape[0]],axis=0)
    zero=jnp.zeros((128,128),F32)
    ahead=[M[8*q:8*q+8,:] for q in range(2)]
    for g in range(8):
        p0=16*g
        if between is not None:
            between(g)
        S=ahead+([M[p0+16+8*q:p0+24+8*q,:] for q in range(2)] if g<7 else [])
        S=sweep(S,0,p0,lane,sub)
        ahead=S[2:]
        R=jnp.concatenate(S[:2],axis=0)
        M=jnp.where((biglane>=p0)&(biglane<p0+16),0.0,M)-mm_inner(M,put(R,p0,zero))
        M=put(R,p0,M)
    return M

def eliminate(mat, between, rest):
    for k in range(4):
        b=128*k
        Mi=invert(mat[b:b+128,b:b+128], between if k==0 else None)
        if k==0:
            rest()
        R=mm(Mi,mat[b:b+128,b+128:])
        order=[(k+1+t)%4 for t in range(3)]
        if k<3:
            o=k+1
            mat[128*o:128*o+128,128*o:128*o+128]-=mm(mat[128*o:128*o+128,b:b+128],R[:,:128])
            mat[128*o:128*o+128,128*o+128:]-=mm(mat[128*o:128*o+128,b:b+128],R[:,128:])
            order=order[1:]
        for o in order:
            mat[128*o:128*o+128,b+128:]-=mm(mat[128*o:128*o+128,b:b+128],R)
        mat[b:b+128,b+128:]=R

def assemble(red_ref, mat, scale, root, ridge, start, stop):
    r=lax.broadcasted_iota(jnp.int32,(128,128),0); c=lax.broadcasted_iota(jnp.int32,(128,128),1)
    for n in range(start,stop):
        i,j=PAIRS[n]
        b=red_ref[128*n:128*n+128,:]*scale
        if i==j: b=b+jnp.where(r==c,ridge,0.0)
        mat[128*i:128*i+128,128*j:128*j+128]=b
        if i!=j: mat[128*j:128*j+128,128*i:128*i+128]=b.T
    if stop==len(PAIRS):
        for i in range(4):
            row=red_ref[1280+i:1281+i,:]*root
            mat[128*i:128*i+128,512:640]=jnp.broadcast_to(row,(128,128)).T

MESH = pl.DeviceIdType.MESH
RING8 = (4, 3, 5, 2, 6, 1, 7)
OUTWARD = tuple((i,) for i in range(8))
HOMEWARD = ((0, 1), (2, 3, 4, 5, 6, 7))
MIDWAY = 3


def fit_kernel(dims, consts, bin_hbm, p_hbm, cyc_hbm, az_hbm, src_hbm, out_ref,
               bin_ref, p_ref, cyc_ref, az_ref, src_ref, in_sem, src_scr, mic_scr, hi_scr, lo_scr,
               part, full, mat, acc_c, acc_x, acc_y, buf_c, buf_x, buf_y, buf_z,
               send_sem, recv_c, recv_x, recv_y, recv_z, grecv_y, grecv_x, grecv_c):
    nx, ny, nz, piece = dims
    x = lax.axis_index("grp")
    row = lax.axis_index("row")
    c = lax.rem(row, 2)
    y = lax.rem(row // 2, ny)
    z = row // (2 * ny)

    def at_c():
        return {"row": row + 1 - 2 * c}

    def at_x(o):
        return {"grp": lax.rem(x + o, nx)}

    def at_y(o):
        return {"row": row + 2 * (lax.rem(y + o, ny) - y)}

    def at_z(o):
        return {"row": row + 2 * ny * (lax.rem(z + o, nz) - z)}

    partners = [at_c()] + [at_x(o) for o in range(1, nx)] + [at_y(o) for o in range(1, ny)]
    partners += [at_z(o) for o in range(1, nz)]
    barrier = pltpu.get_barrier_semaphore()
    for partner in partners:
        pl.semaphore_signal(barrier, inc=1, device_id=partner, device_id_type=MESH)

    loads = []
    for n, (src, dst) in enumerate([(src_hbm, src_ref), (cyc_hbm, cyc_ref), (az_hbm, az_ref), (bin_hbm, bin_ref),
                                    (p_hbm, p_ref)]):
        load = pltpu.make_async_copy(src, dst, in_sem.at[n])
        load.start()
        loads.append(load)
    scale, root, ridge, spacing = consts
    panel_gram(loads, spacing, bin_ref, p_ref, cyc_ref, az_ref, src_ref, part, src_scr, mic_scr, hi_scr, lo_scr)
    pl.semaphore_wait(barrier, len(partners))

    def send(src, dst, ssem, rsem, partner):
        pltpu.make_async_remote_copy(src_ref=src, dst_ref=dst, send_sem=ssem, recv_sem=rsem,
                                     device_id=partner, device_id_type=MESH).start()

    def rows(start, count):
        return pl.ds(pl.multiple_of(start, 8), count)

    def tally(ssem, rsem, count):
        ref = full.at[pl.ds(0, count)]
        return pltpu.make_async_remote_copy(src_ref=ref, dst_ref=ref, send_sem=ssem, recv_sem=rsem,
                                            device_id=at_c(), device_id_type=MESH)

    def arrived(rsem, count):
        tally(send_sem.at[0], rsem, count).wait_recv()

    chunk = piece * nx

    def chunk_of(core, yy):
        return rows((core * ny + yy) * chunk, chunk)

    def piece_of(core, yy, xx):
        return rows(((core * ny + yy) * nx + xx) * piece, piece)

    far = [o for o in RING8 if o < ny] + [0]
    targets = [lax.rem(y + o, ny) for o in far]
    for g, members in enumerate(OUTWARD):
        for i in members:
            send(part.at[chunk_of(1 - c, targets[i])], buf_c.at[i], send_sem.at[0], recv_c.at[g], at_c())
    for g, members in enumerate(OUTWARD):
        arrived(recv_c.at[g], len(members) * chunk)
        for i in members:
            acc_c[i] = part[chunk_of(c, targets[i]), :] + buf_c[i]
        for o in (2, 1, 3):
            for i in members:
                send(acc_c.at[i, rows(lax.rem(x + o, nx) * piece, piece)], buf_x.at[i, o - 1],
                     send_sem.at[1], recv_x.at[g], at_x(o))
    for g, members in enumerate(OUTWARD):
        arrived(recv_x.at[g], len(members) * piece * (nx - 1))
        for i in members:
            total = acc_c[i, rows(x * piece, piece), :]
            for k in range(nx - 1):
                total = total + buf_x[i, k]
            acc_x[i] = total
        for i in members:
            if far[i]:
                send(acc_x.at[i], buf_y.at[far[i] - 1], send_sem.at[2], recv_y.at[0], at_y(far[i]))
    arrived(recv_y.at[0], piece * (ny - 1))
    total = acc_x[ny - 1]
    for k in range(ny - 1):
        total = total + buf_y[k]
    acc_y[...] = total
    for o in RING8:
        send(acc_y, buf_z.at[z], send_sem.at[3], recv_z.at[0], at_z(o))
    buf_z[z] = total
    arrived(recv_z.at[0], piece * (nz - 1))
    total = buf_z[0]
    for k in range(1, nz):
        total = total + buf_z[k]
    mine = full.at[piece_of(c, y, x)]
    mine[...] = total
    for o in RING8:
        send(mine, mine, send_sem.at[4], grecv_y.at[0], at_y(o))
    arrived(grecv_y.at[0], piece * (ny - 1))
    for g, members in enumerate(HOMEWARD):
        for o in (2, 1, 3):
            for yy in members:
                ref = full.at[piece_of(c, yy, x)]
                send(ref, ref, send_sem.at[5], grecv_x.at[g], at_x(o))

    def to_core(g):
        members = HOMEWARD[g]
        arrived(grecv_x.at[g], len(members) * piece * (nx - 1))
        ref = full.at[rows((c * ny + members[0]) * chunk, len(members) * chunk)]
        send(ref, ref, send_sem.at[6], grecv_c.at[g], at_c())

    def landed(g):
        arrived(grecv_c.at[g], len(HOMEWARD[g]) * chunk)

    to_core(0)
    landed(0)
    assemble(full, mat, scale, root, ridge, 0, 1)

    def between(step):
        if step == MIDWAY:
            to_core(1)

    def rest():
        landed(1)
        assemble(full, mat, scale, root, ridge, 1, 10)

    eliminate(mat, between, rest)
    block = mat[pl.ds(pl.multiple_of(x * 128, 128), 128), 512:640]
    out_ref[...] = block.T[0:1, :]
    for n, count in enumerate((chunk * ny, piece * ny * (nx - 1), piece * (ny - 1), piece * (nz - 1), piece * (ny - 1),
                               piece * ny * (nx - 1), chunk * ny)):
        tally(send_sem.at[n], recv_c.at[0], count).wait_send()


def fit(consts, nx, ny, nz, p, cyc, az, b, src):
    n = p.shape[1]
    rows = 1536
    piece = rows // (2 * nx * ny)
    anywhere = pl.BlockSpec(memory_space=pl.ANY)
    dma = pltpu.SemaphoreType.DMA
    v = pltpu.VMEM

    return pl.pallas_call(
        functools.partial(fit_kernel, (nx, ny, nz, piece), consts),
        out_shape=jax.ShapeDtypeStruct((1, 128), F32),
        in_specs=[anywhere] * 5,
        out_specs=pl.BlockSpec(memory_space=pltpu.VMEM),
        scratch_shapes=[
            pltpu.SMEM((1,), jnp.int32), v((1, n), F32), v((1, n), jnp.int32), v((1, n), jnp.int32),
            v((1, S), jnp.int32), dma((5,)),
            v((S, 128), BF), v((16, n), BF), v((S + 16, n), BF), v((S, n), BF),
            v((rows, 128), F32), v((rows, 128), F32), v((512, 640), F32),
            v((ny, piece * nx, 128), F32), v((ny, piece, 128), F32), v((piece, 128), F32),
            v((ny, piece * nx, 128), F32), v((ny, nx - 1, piece, 128), F32), v((ny - 1, piece, 128), F32),
            v((nz, piece, 128), F32),
            dma((7,)), *[dma((ny,))] * 7,
        ],
        name="fit",
        compiler_params=pltpu.CompilerParams(collective_id=0, has_side_effects=True, vmem_limit_bytes=56 << 20),
    )(b, p, cyc, az, src.reshape(1, S))


def shards(mesh, pressure, mic_cycle, mic_azimuth, bin_index, source_cell):
    nx = mesh.shape["grp"]
    ny = 8
    nz = mesh.shape["row"] // (2 * ny)
    count = pressure.shape[1] * nx * mesh.shape["row"]
    consts = (1.0 / count, 1.0 / count**0.5, 0.5, 0.08)
    return fit(consts, nx, ny, nz, pressure, mic_cycle, mic_azimuth, bin_index, source_cell)


def solution(mesh):
    placed = (P(None, ("grp", "row")), P(None, ("grp", "row")), P(None, ("grp", "row")), P(), P())
    return jax.shard_map(
        functools.partial(shards, mesh), mesh=mesh, in_specs=placed, out_specs=P(None, "grp"), check_vma=False
    )
```

```python
import functools

import jax
import jax.numpy as jnp
import numpy as np
from jax import lax
from jax.experimental import pallas as pl
from jax.experimental.pallas import tpu as pltpu
from jax.sharding import PartitionSpec as P

F32 = jnp.float32
BF = jnp.bfloat16
S = 512
NRING = 4096
NAZ = 8192
CROSS = [(i, j) for i in range(4) for j in range(i + 1, 4)]

NT=(((1,),(1,)),((),()))
CHUNK=512
SINE=(6.283185160089467, -41.341655031414675, 81.60100407316348, -76.54978229140988, 39.5367060495799)
MAGIC=12582912.0

def split(v,n):
    parts=[]
    for _ in range(n-1):
        h=v.astype(BF); parts.append(h); v=v-h.astype(F32)
    parts.append(v.astype(BF)); return parts

def cos_turns(t, gain=None):
    y=t-((t+MAGIC)-MAGIC)
    v=0.25-jnp.abs(y)
    u=v*v
    s=SINE[4]
    for c in SINE[3::-1]: s=s*u+c
    return (s*v) if gain is None else s*(v*gain)

def bf16_parts(value, n):
    parts = []
    for _ in range(n):
        part = float(np.float32(value).astype(jnp.bfloat16))
        parts.append(part)
        value -= part
    return parts


UNIT=bf16_parts((1.5/(2*np.pi))**2, 3)
HALF=256


def order_of(bin_ref):
    order = bin_ref[0].astype(F32) + 1.0
    return order * order


def panel_gram(loads, spacing, bin_ref, p_ref, cyc_ref, az_ref, src_ref, out_ref, src_scr, mic_scr, hi_scr, lo_scr):
    loads[0].wait()
    loads[3].wait()
    cell=src_ref[...].astype(F32)
    li=jnp.floor((cell+0.5)*0.01); rest=cell-100.0*li
    lj=jnp.floor((rest+0.5)*0.1); ll=rest-10.0*lj
    t=[2.0*v-9.0 for v in (li,lj,ll)]
    sq=t[0]*t[0]+t[1]*t[1]+t[2]*t[2]
    one=jnp.ones_like(sq); zero=jnp.zeros_like(sq)
    sq_order=one*(order_of(bin_ref))
    rows=[t[0]]*3+[t[1]]*3+[t[2]]*3+[sq]*3+[sq_order]*3
    sT=jnp.concatenate(rows+[zero]*(128-len(rows)),axis=0)
    src_scr[...]=sT.T.astype(BF)
    loads[1].wait()
    loads[2].wait()
    order=bin_ref[0].astype(F32)+1.0
    turns=(order*order)*float((1.5/(2*np.pi))**2)
    half=spacing*0.5
    polar=(2*cyc_ref[...]+1).astype(F32)*(1.0/16384.0)
    azim=az_ref[...].astype(F32)*(1.0/8192.0)
    sp=cos_turns(polar-0.25); cp=cos_turns(polar)
    mic=[sp*cos_turns(azim), sp*cos_turns(azim-0.25), cp]
    mrows=[]
    for m in mic: mrows+=split(m*(turns*(-2.0*half)),3)
    w=jnp.full(mic[0].shape,half*half,F32)*turns
    mrows+=split(w,3)+[jnp.full(w.shape,v,BF) for v in UNIT]
    mrows=[m.astype(F32) for m in mrows]
    mrows+=[jnp.zeros_like(w)]*(16-len(mrows))
    mic_scr[...]=jnp.concatenate(mrows,axis=0).astype(BF)
    n=p_ref.shape[1]
    loads[4].wait()
    ph,pm=[v.astype(F32) for v in split(p_ref[...],2)]
    hi_scr[HALF:HALF+16,:]=jnp.concatenate([ph,pm]+[jnp.zeros_like(ph)]*14,axis=0).astype(BF)
    for lo in range(0, S, HALF):
        for c in range(n//CHUNK):
            cols=slice(c*CHUNK,(c+1)*CHUNK)
            t2=jnp.dot(src_scr[lo:lo+HALF,:16],mic_scr[:,cols],preferred_element_type=F32)
            r=lax.rsqrt(t2)
            val=cos_turns(t2*r, r)
            h=val.astype(BF)
            hi_scr[lo+(16 if lo else 0):lo+(16 if lo else 0)+HALF,cols]=h
            lo_scr[lo:lo+HALF,cols]=(val-h.astype(F32)).astype(BF)
    unit=1.5*(bin_ref[0].astype(F32)+1.0)*float(1/(2*np.pi))
    gain=unit*unit
    def product(a, b):
        return lax.dot_general(a, b, NT, preferred_element_type=F32)
    R0=HALF+16
    H1=product(hi_scr[0:R0],hi_scr[0:HALF]); L1=product(hi_scr[...],lo_scr[0:HALF])
    H2=product(hi_scr[...],hi_scr[R0:]); L2=product(hi_scr[...],lo_scr[HALF:S])
    def at(i):
        return 128*i+(16 if i>=2 else 0)
    def hblk(i,j):
        m=H1 if j<2 else H2
        return m[at(i):at(i)+128,128*(j%2):128*(j%2)+128]
    def lblk(i,j):
        m=L1 if j<2 else L2
        return m[at(i):at(i)+128,128*(j%2):128*(j%2)+128]
    def gram(i,j):
        return ((hblk(i,j)+lblk(i,j))+lblk(j,i).T)*gain
    ri=lax.broadcasted_iota(jnp.int32,(128,128),0); ci=lax.broadcasted_iota(jnp.int32,(128,128),1)
    diagonals=[]
    for n,i in ((0,0),(7,2)):
        other=gram(i+1,i+1)
        out_ref[128*n:128*n+128,:]=jnp.where(ri<=ci,gram(i,i),other)
        diagonals.append(jnp.sum(jnp.where(ri==ci,other,0.0),axis=0,keepdims=True))
    for n,(i,j) in enumerate(CROSS):
        out_ref[128*(n+1):128*(n+1)+128,:]=gram(i,j)
    r1=(H1[HALF:HALF+1]+L1[HALF:HALF+1])+(H1[HALF+1:HALF+2]+L1[HALF+1:HALF+2])
    r2=(H2[HALF:HALF+1]+L2[HALF:HALF+1])+(H2[HALF+1:HALF+2]+L2[HALF+1:HALF+2])
    tail=jnp.concatenate([r1[:,:128],r1[:,128:],r2[:,:128],r2[:,128:]],axis=0)*unit
    out_ref[1024:1032,:]=jnp.concatenate([tail]+diagonals+[jnp.zeros((2,128),F32)],axis=0)

TERMS=6; INNER=3; SG=16
def dot(a,b): return jnp.dot(a,b,preferred_element_type=F32)
def mm(a,b):
    if TERMS==3:
        ah,am=split(a,2); bh,bm=split(b,2)
        return dot(jnp.concatenate([ah,am],1),jnp.concatenate([bh,bh],0))+dot(ah,bm)
    if TERMS==6:
        ah,am,al=split(a,3); bh,bm,bl_=split(b,3)
        ahm=jnp.concatenate([ah,am],1)
        return (dot(jnp.concatenate([ah,al],1),jnp.concatenate([bl_,bh],0))+dot(ahm,jnp.concatenate([bm,bm],0)))+dot(ahm,jnp.concatenate([bh,bh],0))
    if TERMS==1:
        return dot(a.astype(BF),b.astype(BF))
    return jnp.dot(a,b,precision=lax.Precision.HIGHEST,preferred_element_type=F32)

def bl(v,c): return jnp.broadcast_to(v[:,c:c+1],(8,128))
def bs(v,r): return jnp.broadcast_to(v[r:r+1,:],(8,128))

def mm_inner(a,b):
    if INNER==3:
        ah,am=split(a,2); bh,bm=split(b,2)
        return dot(jnp.concatenate([ah,am],1),jnp.concatenate([bh,bh],0))+dot(ah,bm)
    if INNER==6:
        ah,am,al=split(a,3); bh,bm,bl_=split(b,3)
        ahm=jnp.concatenate([ah,am],1)
        return (dot(jnp.concatenate([ah,al],1),jnp.concatenate([bl_,bh],0))+dot(ahm,jnp.concatenate([bm,bm],0)))+dot(ahm,jnp.concatenate([bh,bh],0))
    return jnp.dot(a,b,precision=lax.Precision.HIGHEST,preferred_element_type=F32)

def sweep(S, first, c0, lane, sub):
    nq=len(S)
    B=[jnp.stack([jnp.broadcast_to(S[q][:,c:c+1],(8,128)) for c in range(c0,c0+SG)]) for q in range(nq)]
    piv=(lane>=c0)&(lane<c0+SG)
    for q in range(nq):
        fill=jnp.where(lane-c0==sub+(8*q-first),1.0,0.0) if first<=8*q<first+SG else 0.0
        S[q]=jnp.where(piv,fill,S[q])
    scale=[None]*nq
    for j in range(SG):
        qj,rj=divmod(first+j,8)
        mine=sub==rj
        inv=1.0/jnp.broadcast_to(B[qj][0,rj:rj+1,:],(8,128))
        rawS=S[qj][rj:rj+1,:]
        g=[(jnp.where(mine,0.0,B[q][0]) if q==qj else B[q][0])*inv for q in range(nq)]
        scale[qj]=inv if scale[qj] is None else jnp.where(sub>=rj,inv,scale[qj])
        if j<SG-1:
            raw=B[qj][1:,rj:rj+1,:]
            B=[B[q][1:]-g[q]*raw for q in range(nq)]
        S=[S[q]-g[q]*rawS for q in range(nq)]
    return [S[q] if scale[q] is None else S[q]*scale[q] for q in range(nq)]

def invert(M, between=None):
    lane=lax.broadcasted_iota(jnp.int32,(8,128),1); sub=lax.broadcasted_iota(jnp.int32,(8,128),0)
    biglane=lax.broadcasted_iota(jnp.int32,(128,128),1)
    def put(rows, start, into):
        return jnp.concatenate([x for x in [into[:start],rows,into[start+rows.shape[0]:]] if x.shape[0]],axis=0)
    zero=jnp.zeros((128,128),F32)
    ahead=[M[8*q:8*q+8,:] for q in range(2)]
    for g in range(8):
        p0=16*g
        if between is not None:
            between(g)
        S=ahead+([M[p0+16+8*q:p0+24+8*q,:] for q in range(2)] if g<7 else [])
        S=sweep(S,0,p0,lane,sub)
        ahead=S[2:]
        R=jnp.concatenate(S[:2],axis=0)
        M=jnp.where((biglane>=p0)&(biglane<p0+16),0.0,M)-mm_inner(M,put(R,p0,zero))
        M=put(R,p0,M)
    return M

def eliminate(mat, between, rest):
    for k in range(4):
        b=128*k
        Mi=invert(mat[b:b+128,b:b+128], between if k==0 else None)
        if k==0:
            rest()
        R=mm(Mi,mat[b:b+128,b+128:])
        order=[(k+1+t)%4 for t in range(3)]
        if k<3:
            o=k+1
            mat[128*o:128*o+128,128*o:128*o+128]-=mm(mat[128*o:128*o+128,b:b+128],R[:,:128])
            mat[128*o:128*o+128,128*o+128:]-=mm(mat[128*o:128*o+128,b:b+128],R[:,128:])
            order=order[1:]
        for o in order:
            mat[128*o:128*o+128,b+128:]-=mm(mat[128*o:128*o+128,b:b+128],R)
        mat[b:b+128,b+128:]=R

def assemble(red_ref, last, mat, scale, root, ridge, first):
    r=lax.broadcasted_iota(jnp.int32,(128,128),0); c=lax.broadcasted_iota(jnp.int32,(128,128),1)
    def pair_of(n, diagonal):
        b=red_ref[128*n:128*n+128,:]
        t=b.T
        one=jnp.where(r<=c,b,t); two=jnp.where(r>c,b,jnp.where(r==c,last[diagonal:diagonal+1,:],t))
        return [v*scale+jnp.where(r==c,ridge,0.0) for v in (one,two)]
    if first:
        mat[0:128,0:128]=pair_of(0,4)[0]
        return
    mat[128:256,128:256]=pair_of(0,4)[1]
    mat[256:384,256:384],mat[384:512,384:512]=pair_of(7,5)
    for n,(i,j) in enumerate(CROSS):
        b=red_ref[128*(n+1):128*(n+1)+128,:]*scale
        mat[128*i:128*i+128,128*j:128*j+128]=b
        mat[128*j:128*j+128,128*i:128*i+128]=b.T
    for i in range(4):
        row=last[i:i+1,:]*root
        mat[128*i:128*i+128,512:640]=jnp.broadcast_to(row,(128,128)).T

MESH = pl.DeviceIdType.MESH
RING8 = (4, 3, 5, 2, 6, 1, 7)
OUTWARD = tuple((i,) for i in range(8))
HOMEWARD = ((0, 1), (2, 3, 4, 5, 6, 7))
MIDWAY = 5


def fit_kernel(dims, consts, bin_hbm, p_hbm, cyc_hbm, az_hbm, src_hbm, out_ref,
               bin_ref, p_ref, cyc_ref, az_ref, src_ref, in_sem, src_scr, mic_scr, hi_scr, lo_scr,
               part, full, mat, last, acc_c, acc_e, acc_x, acc_y, buf_c, buf_ec, buf_x, buf_ex, buf_y, buf_z,
               send_sem, recv_e, recv_c, recv_x, recv_y, recv_z, grecv_y, grecv_x, grecv_c):
    nx, ny, nz, piece = dims
    x = lax.axis_index("grp")
    row = lax.axis_index("row")
    c = lax.rem(row, 2)
    y = lax.rem(row // 2, ny)
    z = row // (2 * ny)

    def at_c():
        return {"row": row + 1 - 2 * c}

    def at_x(o):
        return {"grp": lax.rem(x + o, nx)}

    def at_y(o):
        return {"row": row + 2 * (lax.rem(y + o, ny) - y)}

    def at_z(o):
        return {"row": row + 2 * ny * (lax.rem(z + o, nz) - z)}

    partners = [at_c()] + [at_x(o) for o in range(1, nx)] + [at_y(o) for o in range(1, ny)]
    partners += [at_z(o) for o in range(1, nz)]
    barrier = pltpu.get_barrier_semaphore()
    for partner in partners:
        pl.semaphore_signal(barrier, inc=1, device_id=partner, device_id_type=MESH)

    loads = []
    for n, (src, dst) in enumerate([(src_hbm, src_ref), (cyc_hbm, cyc_ref), (az_hbm, az_ref), (bin_hbm, bin_ref),
                                    (p_hbm, p_ref)]):
        load = pltpu.make_async_copy(src, dst, in_sem.at[n])
        load.start()
        loads.append(load)
    scale, root, ridge, spacing = consts
    panel_gram(loads, spacing, bin_ref, p_ref, cyc_ref, az_ref, src_ref, part, src_scr, mic_scr, hi_scr, lo_scr)
    pl.semaphore_wait(barrier, len(partners))

    def send(src, dst, ssem, rsem, partner):
        pltpu.make_async_remote_copy(src_ref=src, dst_ref=dst, send_sem=ssem, recv_sem=rsem,
                                     device_id=partner, device_id_type=MESH).start()

    def rows(start, count):
        return pl.ds(pl.multiple_of(start, 8), count)

    def tally(ssem, rsem, count):
        ref = full.at[pl.ds(0, count)]
        return pltpu.make_async_remote_copy(src_ref=ref, dst_ref=ref, send_sem=ssem, recv_sem=rsem,
                                            device_id=at_c(), device_id_type=MESH)

    def arrived(rsem, count):
        tally(send_sem.at[0], rsem, count).wait_recv()

    chunk = piece * nx

    def chunk_of(core, yy):
        return rows((core * ny + yy) * chunk, chunk)

    def piece_of(core, yy, xx):
        return rows(((core * ny + yy) * nx + xx) * piece, piece)

    far = [o for o in RING8 if o < ny] + [0]
    targets = [lax.rem(y + o, ny) for o in far]
    body = chunk * ny * 2
    extra = part.at[pl.ds(body, 8)]
    send(extra, buf_ec, send_sem.at[0], recv_e.at[0], at_c())
    for g, members in enumerate(OUTWARD):
        for i in members:
            send(part.at[chunk_of(1 - c, targets[i])], buf_c.at[i], send_sem.at[0], recv_c.at[g], at_c())
    arrived(recv_e.at[0], 8)
    acc_e[...] = extra[...] + buf_ec[...]
    buf_ex[x] = acc_e[...]
    for o in (2, 1, 3):
        send(acc_e, buf_ex.at[x], send_sem.at[1], recv_e.at[1], at_x(o))
    for g, members in enumerate(OUTWARD):
        arrived(recv_c.at[g], len(members) * chunk)
        for i in members:
            acc_c[i] = part[chunk_of(c, targets[i]), :] + buf_c[i]
        for o in (2, 1, 3):
            for i in members:
                send(acc_c.at[i, rows(lax.rem(x + o, nx) * piece, piece)], buf_x.at[i, o - 1],
                     send_sem.at[1], recv_x.at[g], at_x(o))
    arrived(recv_e.at[1], 8 * (nx - 1))
    spread = buf_ex[0]
    for k in range(1, nx):
        spread = spread + buf_ex[k]
    for g, members in enumerate(OUTWARD):
        arrived(recv_x.at[g], len(members) * piece * (nx - 1))
        for i in members:
            total = acc_c[i, rows(x * piece, piece), :]
            for k in range(nx - 1):
                total = total + buf_x[i, k]
            if far[i]:
                acc_x[i, 0:piece, :] = total
                acc_x[i, piece:piece + 8, :] = spread
                send(acc_x.at[i], buf_y.at[y], send_sem.at[2], recv_y.at[0], at_y(far[i]))
            else:
                buf_y[y, 0:piece, :] = total
                buf_y[y, piece:piece + 8, :] = spread
    wide = piece + 8
    arrived(recv_y.at[0], wide * (ny - 1))
    total = buf_y[0]
    for k in range(1, ny):
        total = total + buf_y[k]
    acc_y[...] = total
    for o in RING8:
        send(acc_y, buf_z.at[z], send_sem.at[3], recv_z.at[0], at_z(o))
    buf_z[z] = total
    arrived(recv_z.at[0], wide * (nz - 1))
    total = buf_z[0]
    for k in range(1, nz):
        total = total + buf_z[k]
    mine = full.at[piece_of(c, y, x)]
    mine[...] = total[0:piece]
    last[...] = total[piece:wide]
    for o in RING8:
        send(mine, mine, send_sem.at[4], grecv_y.at[0], at_y(o))
    arrived(grecv_y.at[0], piece * (ny - 1))
    for g, members in enumerate(HOMEWARD):
        for o in (2, 1, 3):
            for yy in members:
                ref = full.at[piece_of(c, yy, x)]
                send(ref, ref, send_sem.at[5], grecv_x.at[g], at_x(o))

    def to_core(g):
        members = HOMEWARD[g]
        arrived(grecv_x.at[g], len(members) * piece * (nx - 1))
        ref = full.at[rows((c * ny + members[0]) * chunk, len(members) * chunk)]
        send(ref, ref, send_sem.at[6], grecv_c.at[g], at_c())

    def landed(g):
        arrived(grecv_c.at[g], len(HOMEWARD[g]) * chunk)

    to_core(0)
    landed(0)
    assemble(full, last, mat, scale, root, ridge, True)

    def between(step):
        if step == MIDWAY:
            to_core(1)

    def rest():
        landed(1)
        assemble(full, last, mat, scale, root, ridge, False)

    eliminate(mat, between, rest)
    block = mat[pl.ds(pl.multiple_of(x * 128, 128), 128), 512:640]
    out_ref[...] = block.T[0:1, :]
    for n, count in enumerate((chunk * ny + 8, (piece * ny + 8) * (nx - 1), wide * (ny - 1), wide * (nz - 1), piece * (ny - 1),
                               piece * ny * (nx - 1), chunk * ny)):
        tally(send_sem.at[n], recv_c.at[0], count).wait_send()


def fit(consts, nx, ny, nz, p, cyc, az, b, src):
    n = p.shape[1]
    rows = 1024
    piece = rows // (2 * nx * ny)
    anywhere = pl.BlockSpec(memory_space=pl.ANY)
    dma = pltpu.SemaphoreType.DMA
    v = pltpu.VMEM

    return pl.pallas_call(
        functools.partial(fit_kernel, (nx, ny, nz, piece), consts),
        out_shape=jax.ShapeDtypeStruct((1, 128), F32),
        in_specs=[anywhere] * 5,
        out_specs=pl.BlockSpec(memory_space=pltpu.VMEM),
        scratch_shapes=[
            pltpu.SMEM((1,), jnp.int32), v((1, n), F32), v((1, n), jnp.int32), v((1, n), jnp.int32),
            v((1, S), jnp.int32), dma((5,)),
            v((S, 128), BF), v((16, n), BF), v((S + 16, n), BF), v((S, n), BF),
            v((rows + 8, 128), F32), v((rows, 128), F32), v((512, 640), F32), v((8, 128), F32),
            v((ny, piece * nx, 128), F32), v((8, 128), F32), v((ny, piece + 8, 128), F32), v((piece + 8, 128), F32),
            v((ny, piece * nx, 128), F32), v((8, 128), F32), v((ny, nx - 1, piece, 128), F32), v((nx, 8, 128), F32),
            v((ny, piece + 8, 128), F32), v((nz, piece + 8, 128), F32),
            dma((7,)), dma((2,)), *[dma((ny,))] * 7,
        ],
        name="fit",
        compiler_params=pltpu.CompilerParams(collective_id=0, has_side_effects=True, vmem_limit_bytes=56 << 20),
    )(b, p, cyc, az, src.reshape(1, S))


def shards(mesh, pressure, mic_cycle, mic_azimuth, bin_index, source_cell):
    nx = mesh.shape["grp"]
    ny = 8
    nz = mesh.shape["row"] // (2 * ny)
    count = pressure.shape[1] * nx * mesh.shape["row"]
    consts = (1.0 / count, 1.0 / count**0.5, 0.5, 0.08)
    return fit(consts, nx, ny, nz, pressure, mic_cycle, mic_azimuth, bin_index, source_cell)


def solution(mesh):
    placed = (P(None, ("grp", "row")), P(None, ("grp", "row")), P(None, ("grp", "row")), P(), P())
    return jax.shard_map(
        functools.partial(shards, mesh), mesh=mesh, in_specs=placed, out_specs=P(None, "grp"), check_vma=False
    )
```

```python
import functools

import jax
import jax.numpy as jnp
import numpy as np
from jax import lax
from jax.experimental import pallas as pl
from jax.experimental.pallas import tpu as pltpu
from jax.sharding import PartitionSpec as P

F32 = jnp.float32
BF = jnp.bfloat16
S = 512
NRING = 4096
NAZ = 8192
CROSS = [(i, j) for i in range(4) for j in range(i + 1, 4)]

NT=(((1,),(1,)),((),()))
CHUNK=512
SINE=(6.283185160089467, -41.341655031414675, 81.60100407316348, -76.54978229140988, 39.5367060495799)
MAGIC=12582912.0

def split(v,n):
    parts=[]
    for _ in range(n-1):
        h=v.astype(BF); parts.append(h); v=v-h.astype(F32)
    parts.append(v.astype(BF)); return parts

def cos_turns(t, gain=None):
    y=t-((t+MAGIC)-MAGIC)
    v=0.25-jnp.abs(y)
    u=v*v
    s=SINE[4]
    for c in SINE[3::-1]: s=s*u+c
    return (s*v) if gain is None else s*(v*gain)

def bf16_parts(value, n):
    parts = []
    for _ in range(n):
        part = float(np.float32(value).astype(jnp.bfloat16))
        parts.append(part)
        value -= part
    return parts


UNIT=bf16_parts((1.5/(2*np.pi))**2, 3)
HALF=256


def order_of(bin_ref):
    order = bin_ref[0].astype(F32) + 1.0
    return order * order


def panel_gram(loads, spacing, bin_ref, p_ref, cyc_ref, az_ref, src_ref, out_ref, src_scr, mic_scr, hi_scr, lo_scr):
    loads[0].wait()
    loads[3].wait()
    cell=src_ref[...].astype(F32)
    li=jnp.floor((cell+0.5)*0.01); rest=cell-100.0*li
    lj=jnp.floor((rest+0.5)*0.1); ll=rest-10.0*lj
    t=[2.0*v-9.0 for v in (li,lj,ll)]
    sq=t[0]*t[0]+t[1]*t[1]+t[2]*t[2]
    one=jnp.ones_like(sq); zero=jnp.zeros_like(sq)
    sq_order=one*(order_of(bin_ref))
    rows=[t[0]]*3+[t[1]]*3+[t[2]]*3+[sq]*3+[sq_order]*3
    sT=jnp.concatenate(rows+[zero]*(128-len(rows)),axis=0)
    src_scr[...]=sT.T.astype(BF)
    loads[1].wait()
    loads[2].wait()
    order=bin_ref[0].astype(F32)+1.0
    turns=(order*order)*float((1.5/(2*np.pi))**2)
    half=spacing*0.5
    polar=(2*cyc_ref[...]+1).astype(F32)*(1.0/16384.0)
    azim=az_ref[...].astype(F32)*(1.0/8192.0)
    sp=cos_turns(polar-0.25); cp=cos_turns(polar)
    mic=[sp*cos_turns(azim), sp*cos_turns(azim-0.25), cp]
    mrows=[]
    for m in mic: mrows+=split(m*(turns*(-2.0*half)),3)
    w=jnp.full(mic[0].shape,half*half,F32)*turns
    mrows+=split(w,3)+[jnp.full(w.shape,v,BF) for v in UNIT]
    mrows=[m.astype(F32) for m in mrows]
    mrows+=[jnp.zeros_like(w)]*(16-len(mrows))
    mic_scr[...]=jnp.concatenate(mrows,axis=0).astype(BF)
    n=p_ref.shape[1]
    loads[4].wait()
    ph,pm=[v.astype(F32) for v in split(p_ref[...],2)]
    hi_scr[HALF:HALF+16,:]=jnp.concatenate([ph,pm]+[jnp.zeros_like(ph)]*14,axis=0).astype(BF)
    for lo in range(0, S, HALF):
        for c in range(n//CHUNK):
            cols=slice(c*CHUNK,(c+1)*CHUNK)
            t2=jnp.dot(src_scr[lo:lo+HALF,:16],mic_scr[:,cols],preferred_element_type=F32)
            r=lax.rsqrt(t2)
            val=cos_turns(t2*r, r)
            h=val.astype(BF)
            hi_scr[lo+(16 if lo else 0):lo+(16 if lo else 0)+HALF,cols]=h
            lo_scr[lo:lo+HALF,cols]=(val-h.astype(F32)).astype(BF)
    unit=1.5*(bin_ref[0].astype(F32)+1.0)*float(1/(2*np.pi))
    gain=unit*unit
    def product(a, b):
        return lax.dot_general(a, b, NT, preferred_element_type=F32)
    R0=HALF+16
    H1=product(hi_scr[0:R0],hi_scr[0:HALF]); L1=product(hi_scr[...],lo_scr[0:HALF])
    H2=product(hi_scr[...],hi_scr[R0:]); L2=product(hi_scr[...],lo_scr[HALF:S])
    def at(i):
        return 128*i+(16 if i>=2 else 0)
    def hblk(i,j):
        m=H1 if j<2 else H2
        return m[at(i):at(i)+128,128*(j%2):128*(j%2)+128]
    def lblk(i,j):
        m=L1 if j<2 else L2
        return m[at(i):at(i)+128,128*(j%2):128*(j%2)+128]
    def gram(i,j):
        return ((hblk(i,j)+lblk(i,j))+lblk(j,i).T)*gain
    ri=lax.broadcasted_iota(jnp.int32,(128,128),0); ci=lax.broadcasted_iota(jnp.int32,(128,128),1)
    diagonals=[]
    for n,i in ((0,0),(7,2)):
        other=gram(i+1,i+1)
        out_ref[128*n:128*n+128,:]=jnp.where(ri<=ci,gram(i,i),other)
        diagonals.append(jnp.sum(jnp.where(ri==ci,other,0.0),axis=0,keepdims=True))
    for n,(i,j) in enumerate(CROSS):
        out_ref[128*(n+1):128*(n+1)+128,:]=gram(i,j)
    r1=(H1[HALF:HALF+1]+L1[HALF:HALF+1])+(H1[HALF+1:HALF+2]+L1[HALF+1:HALF+2])
    r2=(H2[HALF:HALF+1]+L2[HALF:HALF+1])+(H2[HALF+1:HALF+2]+L2[HALF+1:HALF+2])
    tail=jnp.concatenate([r1[:,:128],r1[:,128:],r2[:,:128],r2[:,128:]],axis=0)*unit
    out_ref[1024:1032,:]=jnp.concatenate([tail]+diagonals+[jnp.zeros((2,128),F32)],axis=0)

TERMS=6; INNER=3; SG=16
def dot(a,b): return jnp.dot(a,b,preferred_element_type=F32)
def mm(a,b):
    if TERMS==3:
        ah,am=split(a,2); bh,bm=split(b,2)
        return dot(jnp.concatenate([ah,am],1),jnp.concatenate([bh,bh],0))+dot(ah,bm)
    if TERMS==6:
        ah,am,al=split(a,3); bh,bm,bl_=split(b,3)
        ahm=jnp.concatenate([ah,am],1)
        return (dot(jnp.concatenate([ah,al],1),jnp.concatenate([bl_,bh],0))+dot(ahm,jnp.concatenate([bm,bm],0)))+dot(ahm,jnp.concatenate([bh,bh],0))
    if TERMS==1:
        return dot(a.astype(BF),b.astype(BF))
    return jnp.dot(a,b,precision=lax.Precision.HIGHEST,preferred_element_type=F32)

def bl(v,c): return jnp.broadcast_to(v[:,c:c+1],(8,128))
def bs(v,r): return jnp.broadcast_to(v[r:r+1,:],(8,128))

def mm_inner(a,b):
    if INNER==3:
        ah,am=split(a,2); bh,bm=split(b,2)
        return dot(jnp.concatenate([ah,am],1),jnp.concatenate([bh,bh],0))+dot(ah,bm)
    if INNER==6:
        ah,am,al=split(a,3); bh,bm,bl_=split(b,3)
        ahm=jnp.concatenate([ah,am],1)
        return (dot(jnp.concatenate([ah,al],1),jnp.concatenate([bl_,bh],0))+dot(ahm,jnp.concatenate([bm,bm],0)))+dot(ahm,jnp.concatenate([bh,bh],0))
    return jnp.dot(a,b,precision=lax.Precision.HIGHEST,preferred_element_type=F32)

def sweep(S, first, c0, lane, sub):
    nq=len(S)
    B=[jnp.stack([jnp.broadcast_to(S[q][:,c:c+1],(8,128)) for c in range(c0,c0+SG)]) for q in range(nq)]
    piv=(lane>=c0)&(lane<c0+SG)
    for q in range(nq):
        fill=jnp.where(lane-c0==sub+(8*q-first),1.0,0.0) if first<=8*q<first+SG else 0.0
        S[q]=jnp.where(piv,fill,S[q])
    scale=[None]*nq
    for j in range(SG):
        qj,rj=divmod(first+j,8)
        mine=sub==rj
        inv=1.0/jnp.broadcast_to(B[qj][0,rj:rj+1,:],(8,128))
        rawS=S[qj][rj:rj+1,:]
        g=[(jnp.where(mine,0.0,B[q][0]) if q==qj else B[q][0])*inv for q in range(nq)]
        scale[qj]=inv if scale[qj] is None else jnp.where(sub>=rj,inv,scale[qj])
        if j<SG-1:
            raw=B[qj][1:,rj:rj+1,:]
            B=[B[q][1:]-g[q]*raw for q in range(nq)]
        S=[S[q]-g[q]*rawS for q in range(nq)]
    return [S[q] if scale[q] is None else S[q]*scale[q] for q in range(nq)]

def invert(M, between=None):
    lane=lax.broadcasted_iota(jnp.int32,(8,128),1); sub=lax.broadcasted_iota(jnp.int32,(8,128),0)
    biglane=lax.broadcasted_iota(jnp.int32,(128,128),1)
    def put(rows, start, into):
        return jnp.concatenate([x for x in [into[:start],rows,into[start+rows.shape[0]:]] if x.shape[0]],axis=0)
    zero=jnp.zeros((128,128),F32)
    ahead=[M[8*q:8*q+8,:] for q in range(2)]
    for g in range(8):
        p0=16*g
        if between is not None:
            between(g)
        S=ahead+([M[p0+16+8*q:p0+24+8*q,:] for q in range(2)] if g<7 else [])
        S=sweep(S,0,p0,lane,sub)
        ahead=S[2:]
        R=jnp.concatenate(S[:2],axis=0)
        M=jnp.where((biglane>=p0)&(biglane<p0+16),0.0,M)-mm_inner(M,put(R,p0,zero))
        M=put(R,p0,M)
    return M

def eliminate(mat, between, rest):
    for k in range(4):
        b=128*k
        Mi=invert(mat[b:b+128,b:b+128], between if k==0 else None)
        if k==0:
            rest()
        R=mm(Mi,mat[b:b+128,b+128:])
        order=[(k+1+t)%4 for t in range(3)]
        if k<3:
            o=k+1
            mat[128*o:128*o+128,128*o:128*o+128]-=mm(mat[128*o:128*o+128,b:b+128],R[:,:128])
            mat[128*o:128*o+128,128*o+128:]-=mm(mat[128*o:128*o+128,b:b+128],R[:,128:])
            order=order[1:]
        for o in order:
            mat[128*o:128*o+128,b+128:]-=mm(mat[128*o:128*o+128,b:b+128],R)
        mat[b:b+128,b+128:]=R

def assemble(red_ref, last, mat, scale, root, ridge, first):
    r=lax.broadcasted_iota(jnp.int32,(128,128),0); c=lax.broadcasted_iota(jnp.int32,(128,128),1)
    def pair_of(n, diagonal):
        b=red_ref[128*n:128*n+128,:]
        t=b.T
        one=jnp.where(r<=c,b,t); two=jnp.where(r>c,b,jnp.where(r==c,last[diagonal:diagonal+1,:],t))
        return [v*scale+jnp.where(r==c,ridge,0.0) for v in (one,two)]
    if first:
        mat[0:128,0:128]=pair_of(0,4)[0]
        return
    mat[128:256,128:256]=pair_of(0,4)[1]
    mat[256:384,256:384],mat[384:512,384:512]=pair_of(7,5)
    for n,(i,j) in enumerate(CROSS):
        b=red_ref[128*(n+1):128*(n+1)+128,:]*scale
        mat[128*i:128*i+128,128*j:128*j+128]=b
        mat[128*j:128*j+128,128*i:128*i+128]=b.T
    for i in range(4):
        row=last[i:i+1,:]*root
        mat[128*i:128*i+128,512:640]=jnp.broadcast_to(row,(128,128)).T

MESH = pl.DeviceIdType.MESH
RING8 = (4, 3, 5, 2, 6, 1, 7)
OUTWARD = tuple((i,) for i in range(8))
HOMEWARD = ((0, 1), (2, 3, 4, 5, 6, 7))
MIDWAY = 6


def fit_kernel(dims, consts, bin_hbm, p_hbm, cyc_hbm, az_hbm, src_hbm, out_ref,
               bin_ref, p_ref, cyc_ref, az_ref, src_ref, in_sem, src_scr, mic_scr, hi_scr, lo_scr,
               part, full, mat, last, acc_c, acc_e, acc_x, acc_y, buf_c, buf_ec, buf_x, buf_ex, buf_y, buf_z,
               send_sem, recv_e, recv_c, recv_x, recv_y, recv_z, grecv_y, grecv_x, grecv_c):
    nx, ny, nz, piece = dims
    x = lax.axis_index("grp")
    row = lax.axis_index("row")
    c = lax.rem(row, 2)
    y = lax.rem(row // 2, ny)
    z = row // (2 * ny)

    def at_c():
        return {"row": row + 1 - 2 * c}

    def at_x(o):
        return {"grp": lax.rem(x + o, nx)}

    def at_y(o):
        return {"row": row + 2 * (lax.rem(y + o, ny) - y)}

    def at_z(o):
        return {"row": row + 2 * ny * (lax.rem(z + o, nz) - z)}

    partners = [{"grp": lax.rem(x + o, nx), "row": row + 1 - 2 * c} for o in range(nx)] + [at_x(o) for o in range(1, nx)] + [at_y(o) for o in range(1, ny)]
    partners += [at_z(o) for o in range(1, nz)]
    barrier = pltpu.get_barrier_semaphore()
    for partner in partners:
        pl.semaphore_signal(barrier, inc=1, device_id=partner, device_id_type=MESH)

    loads = []
    for n, (src, dst) in enumerate([(src_hbm, src_ref), (cyc_hbm, cyc_ref), (az_hbm, az_ref), (bin_hbm, bin_ref),
                                    (p_hbm, p_ref)]):
        load = pltpu.make_async_copy(src, dst, in_sem.at[n])
        load.start()
        loads.append(load)
    scale, root, ridge, spacing = consts
    panel_gram(loads, spacing, bin_ref, p_ref, cyc_ref, az_ref, src_ref, part, src_scr, mic_scr, hi_scr, lo_scr)
    pl.semaphore_wait(barrier, len(partners))

    def send(src, dst, ssem, rsem, partner):
        pltpu.make_async_remote_copy(src_ref=src, dst_ref=dst, send_sem=ssem, recv_sem=rsem,
                                     device_id=partner, device_id_type=MESH).start()

    def rows(start, count):
        return pl.ds(pl.multiple_of(start, 8), count)

    def tally(ssem, rsem, count):
        ref = full.at[pl.ds(0, count)]
        return pltpu.make_async_remote_copy(src_ref=ref, dst_ref=ref, send_sem=ssem, recv_sem=rsem,
                                            device_id=at_c(), device_id_type=MESH)

    def arrived(rsem, count):
        tally(send_sem.at[0], rsem, count).wait_recv()

    chunk = piece * nx

    def chunk_of(core, yy):
        return rows((core * ny + yy) * chunk, chunk)

    def piece_of(core, yy, xx):
        return rows(((core * ny + yy) * nx + xx) * piece, piece)

    far = [o for o in RING8 if o < ny] + [0]
    targets = [lax.rem(y + o, ny) for o in far]
    body = chunk * ny * 2
    extra = part.at[pl.ds(body, 8)]
    send(extra, buf_ec, send_sem.at[0], recv_e.at[0], at_c())
    for g, members in enumerate(OUTWARD):
        for i in members:
            send(part.at[chunk_of(1 - c, targets[i])], buf_c.at[i], send_sem.at[0], recv_c.at[g], at_c())
    arrived(recv_e.at[0], 8)
    acc_e[...] = extra[...] + buf_ec[...]
    buf_ex[x] = acc_e[...]
    for o in (2, 1, 3):
        send(acc_e, buf_ex.at[x], send_sem.at[1], recv_e.at[1], at_x(o))
    for g, members in enumerate(OUTWARD):
        arrived(recv_c.at[g], len(members) * chunk)
        for i in members:
            acc_c[i] = part[chunk_of(c, targets[i]), :] + buf_c[i]
        for o in (2, 1, 3):
            for i in members:
                send(acc_c.at[i, rows(lax.rem(x + o, nx) * piece, piece)], buf_x.at[i, o - 1],
                     send_sem.at[1], recv_x.at[g], at_x(o))
    arrived(recv_e.at[1], 8 * (nx - 1))
    spread = buf_ex[0]
    for k in range(1, nx):
        spread = spread + buf_ex[k]
    for g, members in enumerate(OUTWARD):
        arrived(recv_x.at[g], len(members) * piece * (nx - 1))
        for i in members:
            total = acc_c[i, rows(x * piece, piece), :]
            for k in range(nx - 1):
                total = total + buf_x[i, k]
            if far[i]:
                acc_x[i, 0:piece, :] = total
                acc_x[i, piece:piece + 8, :] = spread
                send(acc_x.at[i], buf_y.at[y], send_sem.at[2], recv_y.at[0], at_y(far[i]))
            else:
                buf_y[y, 0:piece, :] = total
                buf_y[y, piece:piece + 8, :] = spread
    wide = piece + 8
    arrived(recv_y.at[0], wide * (ny - 1))
    total = buf_y[0]
    for k in range(1, ny):
        total = total + buf_y[k]
    acc_y[...] = total
    for o in RING8:
        send(acc_y, buf_z.at[z], send_sem.at[3], recv_z.at[0], at_z(o))
    buf_z[z] = total
    arrived(recv_z.at[0], wide * (nz - 1))
    total = buf_z[0]
    for k in range(1, nz):
        total = total + buf_z[k]
    mine = full.at[piece_of(c, y, x)]
    mine[...] = total[0:piece]
    last[...] = total[piece:wide]
    for o in RING8:
        send(mine, mine, send_sem.at[4], grecv_y.at[o - 1], at_y(o))
    early = len(HOMEWARD[0])
    for o in (0,) + RING8[::-1]:
        if o:
            arrived(grecv_y.at[o - 1], piece)
        source = lax.rem(y - o + ny, ny)
        ref = full.at[piece_of(c, source, x)]
        group = (source + ny - early) // ny
        for k in (2, 1, 3):
            send(ref, ref, send_sem.at[5], grecv_x.at[group], at_x(k))

        @pl.when(source < early)
        def _():
            for k in (2, 1, 3, 0):
                across = {"grp": lax.rem(x + k, nx), "row": row + 1 - 2 * c}
                send(ref, ref, send_sem.at[5], grecv_x.at[0], across)

    def to_core(g):
        members = HOMEWARD[g]
        arrived(grecv_x.at[g], len(members) * piece * (nx - 1))
        ref = full.at[rows((c * ny + members[0]) * chunk, len(members) * chunk)]
        send(ref, ref, send_sem.at[6], grecv_c.at[g], at_c())

    def landed(g):
        arrived(grecv_c.at[g], len(HOMEWARD[g]) * chunk)

    arrived(grecv_x.at[0], early * piece * (2 * nx - 1))
    assemble(full, last, mat, scale, root, ridge, True)

    def between(step):
        if step == MIDWAY:
            to_core(1)

    def rest():
        landed(1)
        assemble(full, last, mat, scale, root, ridge, False)

    eliminate(mat, between, rest)
    block = mat[pl.ds(pl.multiple_of(x * 128, 128), 128), 512:640]
    out_ref[...] = block.T[0:1, :]
    for n, count in enumerate((chunk * ny + 8, (piece * ny + 8) * (nx - 1), wide * (ny - 1), wide * (nz - 1), piece * (ny - 1),
                               piece * (ny * (nx - 1) + early * nx), chunk * (ny - early))):
        tally(send_sem.at[n], recv_c.at[0], count).wait_send()


def fit(consts, nx, ny, nz, p, cyc, az, b, src):
    n = p.shape[1]
    rows = 1024
    piece = rows // (2 * nx * ny)
    anywhere = pl.BlockSpec(memory_space=pl.ANY)
    dma = pltpu.SemaphoreType.DMA
    v = pltpu.VMEM

    return pl.pallas_call(
        functools.partial(fit_kernel, (nx, ny, nz, piece), consts),
        out_shape=jax.ShapeDtypeStruct((1, 128), F32),
        in_specs=[anywhere] * 5,
        out_specs=pl.BlockSpec(memory_space=pltpu.VMEM),
        scratch_shapes=[
            pltpu.SMEM((1,), jnp.int32), v((1, n), F32), v((1, n), jnp.int32), v((1, n), jnp.int32),
            v((1, S), jnp.int32), dma((5,)),
            v((S, 128), BF), v((16, n), BF), v((S + 16, n), BF), v((S, n), BF),
            v((rows + 8, 128), F32), v((rows, 128), F32), v((512, 640), F32), v((8, 128), F32),
            v((ny, piece * nx, 128), F32), v((8, 128), F32), v((ny, piece + 8, 128), F32), v((piece + 8, 128), F32),
            v((ny, piece * nx, 128), F32), v((8, 128), F32), v((ny, nx - 1, piece, 128), F32), v((nx, 8, 128), F32),
            v((ny, piece + 8, 128), F32), v((nz, piece + 8, 128), F32),
            dma((7,)), dma((2,)), *[dma((ny,))] * 7,
        ],
        name="fit",
        compiler_params=pltpu.CompilerParams(collective_id=0, has_side_effects=True, vmem_limit_bytes=56 << 20),
    )(b, p, cyc, az, src.reshape(1, S))


def shards(mesh, pressure, mic_cycle, mic_azimuth, bin_index, source_cell):
    nx = mesh.shape["grp"]
    ny = 8
    nz = mesh.shape["row"] // (2 * ny)
    count = pressure.shape[1] * nx * mesh.shape["row"]
    consts = (1.0 / count, 1.0 / count**0.5, 0.5, 0.08)
    return fit(consts, nx, ny, nz, pressure, mic_cycle, mic_azimuth, bin_index, source_cell)


def solution(mesh):
    placed = (P(None, ("grp", "row")), P(None, ("grp", "row")), P(None, ("grp", "row")), P(), P())
    return jax.shard_map(
        functools.partial(shards, mesh), mesh=mesh, in_specs=placed, out_specs=P(None, "grp"), check_vma=False
    )
```

```python
import functools

import jax
import jax.numpy as jnp
import numpy as np
from jax import lax
from jax.experimental import pallas as pl
from jax.experimental.pallas import tpu as pltpu
from jax.sharding import PartitionSpec as P

F32 = jnp.float32
BF = jnp.bfloat16
S = 512
NRING = 4096
NAZ = 8192
CROSS = [(i, j) for i in range(4) for j in range(i + 1, 4)]

NT=(((1,),(1,)),((),()))
CHUNK=256
SINE=(6.283185160089467, -41.341655031414675, 81.60100407316348, -76.54978229140988, 39.5367060495799)
MAGIC=12582912.0

def split(v,n):
    parts=[]
    for _ in range(n-1):
        h=v.astype(BF); parts.append(h); v=v-h.astype(F32)
    parts.append(v.astype(BF)); return parts

def cos_turns(t, gain=None):
    y=t-((t+MAGIC)-MAGIC)
    v=0.25-jnp.abs(y)
    u=v*v
    s=SINE[4]
    for c in SINE[3::-1]: s=s*u+c
    return (s*v) if gain is None else s*(v*gain)

def bf16_parts(value, n):
    parts = []
    for _ in range(n):
        part = float(np.float32(value).astype(jnp.bfloat16))
        parts.append(part)
        value -= part
    return parts


UNIT=bf16_parts((1.5/(2*np.pi))**2, 3)
HALF=256


def order_of(bin_ref):
    order = bin_ref[0].astype(F32) + 1.0
    return order * order


def panel_gram(loads, spacing, bin_ref, p_ref, cyc_ref, az_ref, src_ref, out_ref, src_scr, mic_scr, hi_scr, lo_scr):
    loads[0].wait()
    loads[3].wait()
    cell=src_ref[...].astype(F32)
    li=jnp.floor((cell+0.5)*0.01); rest=cell-100.0*li
    lj=jnp.floor((rest+0.5)*0.1); ll=rest-10.0*lj
    t=[2.0*v-9.0 for v in (li,lj,ll)]
    sq=t[0]*t[0]+t[1]*t[1]+t[2]*t[2]
    one=jnp.ones_like(sq); zero=jnp.zeros_like(sq)
    sq_order=one*(order_of(bin_ref))
    rows=[t[0]]*3+[t[1]]*3+[t[2]]*3+[sq]*3+[sq_order]*3
    sT=jnp.concatenate(rows+[zero]*(128-len(rows)),axis=0)
    src_scr[...]=sT.T.astype(BF)
    loads[1].wait()
    loads[2].wait()
    order=bin_ref[0].astype(F32)+1.0
    turns=(order*order)*float((1.5/(2*np.pi))**2)
    half=spacing*0.5
    polar=(2*cyc_ref[...]+1).astype(F32)*(1.0/16384.0)
    azim=az_ref[...].astype(F32)*(1.0/8192.0)
    sp=cos_turns(polar-0.25); cp=cos_turns(polar)
    mic=[sp*cos_turns(azim), sp*cos_turns(azim-0.25), cp]
    mrows=[]
    for m in mic: mrows+=split(m*(turns*(-2.0*half)),3)
    w=jnp.full(mic[0].shape,half*half,F32)*turns
    mrows+=split(w,3)+[jnp.full(w.shape,v,BF) for v in UNIT]
    mrows=[m.astype(F32) for m in mrows]
    mrows+=[jnp.zeros_like(w)]*(16-len(mrows))
    mic_scr[...]=jnp.concatenate(mrows,axis=0).astype(BF)
    n=p_ref.shape[1]
    loads[4].wait()
    ph,pm=[v.astype(F32) for v in split(p_ref[...],2)]
    hi_scr[HALF:HALF+16,:]=jnp.concatenate([ph,pm]+[jnp.zeros_like(ph)]*14,axis=0).astype(BF)
    def fill(lo, c):
        cols=slice(c*CHUNK,(c+1)*CHUNK)
        t2=jnp.dot(src_scr[lo:lo+HALF,:16],mic_scr[:,cols],preferred_element_type=F32)
        r=lax.rsqrt(t2)
        val=cos_turns(t2*r, r)
        h=val.astype(BF)
        base=lo+(16 if lo else 0)
        hi_scr[base:base+HALF,cols]=h
        lo_scr[lo:lo+HALF,cols]=(val-h.astype(F32)).astype(BF)
    def product(a, b):
        return lax.dot_general(a, b, NT, preferred_element_type=F32)
    R0=HALF+16
    unit=1.5*(bin_ref[0].astype(F32)+1.0)*float(1/(2*np.pi))
    gain=unit*unit
    H1=L1=H2=L2=None
    for c in range(n//CHUNK+1):
        if c<n//CHUNK:
            fill(0, c); fill(HALF, c)
        if c:
            k=slice((c-1)*CHUNK,c*CHUNK)
            new=[product(hi_scr[0:R0,k],hi_scr[0:HALF,k]),product(hi_scr[:,k],lo_scr[0:HALF,k]),product(hi_scr[:,k],hi_scr[R0:,k]),product(hi_scr[:,k],lo_scr[HALF:S,k])]
            if H1 is not None: new=[u+v for u,v in zip((H1,L1,H2,L2),new)]
            H1,L1,H2,L2=new
    def at(i):
        return 128*i+(16 if i>=2 else 0)
    def hblk(i,j):
        m=H1 if j<2 else H2
        return m[at(i):at(i)+128,128*(j%2):128*(j%2)+128]
    def lblk(i,j):
        m=L1 if j<2 else L2
        return m[at(i):at(i)+128,128*(j%2):128*(j%2)+128]
    def gram(i,j):
        return ((hblk(i,j)+lblk(i,j))+lblk(j,i).T)*gain
    ri=lax.broadcasted_iota(jnp.int32,(128,128),0); ci=lax.broadcasted_iota(jnp.int32,(128,128),1)
    diagonals=[]
    for n,i in ((0,0),(7,2)):
        other=gram(i+1,i+1)
        out_ref[128*n:128*n+128,:]=jnp.where(ri<=ci,gram(i,i),other)
        diagonals.append(jnp.sum(jnp.where(ri==ci,other,0.0),axis=0,keepdims=True))
    for n,(i,j) in enumerate(CROSS):
        out_ref[128*(n+1):128*(n+1)+128,:]=gram(i,j)
    r1=(H1[HALF:HALF+1]+L1[HALF:HALF+1])+(H1[HALF+1:HALF+2]+L1[HALF+1:HALF+2])
    r2=(H2[HALF:HALF+1]+L2[HALF:HALF+1])+(H2[HALF+1:HALF+2]+L2[HALF+1:HALF+2])
    tail=jnp.concatenate([r1[:,:128],r1[:,128:],r2[:,:128],r2[:,128:]],axis=0)*unit
    out_ref[1024:1032,:]=jnp.concatenate([tail]+diagonals+[jnp.zeros((2,128),F32)],axis=0)

TERMS=6; INNER=3; SG=16
def dot(a,b): return jnp.dot(a,b,preferred_element_type=F32)
def mm(a,b):
    if TERMS==3:
        ah,am=split(a,2); bh,bm=split(b,2)
        return dot(jnp.concatenate([ah,am],1),jnp.concatenate([bh,bh],0))+dot(ah,bm)
    if TERMS==6:
        ah,am,al=split(a,3); bh,bm,bl_=split(b,3)
        ahm=jnp.concatenate([ah,am],1)
        return (dot(jnp.concatenate([ah,al],1),jnp.concatenate([bl_,bh],0))+dot(ahm,jnp.concatenate([bm,bm],0)))+dot(ahm,jnp.concatenate([bh,bh],0))
    if TERMS==1:
        return dot(a.astype(BF),b.astype(BF))
    return jnp.dot(a,b,precision=lax.Precision.HIGHEST,preferred_element_type=F32)

def bl(v,c): return jnp.broadcast_to(v[:,c:c+1],(8,128))
def bs(v,r): return jnp.broadcast_to(v[r:r+1,:],(8,128))

def mm_inner(a,b):
    if INNER==3:
        ah,am=split(a,2); bh,bm=split(b,2)
        return dot(jnp.concatenate([ah,am],1),jnp.concatenate([bh,bh],0))+dot(ah,bm)
    if INNER==6:
        ah,am,al=split(a,3); bh,bm,bl_=split(b,3)
        ahm=jnp.concatenate([ah,am],1)
        return (dot(jnp.concatenate([ah,al],1),jnp.concatenate([bl_,bh],0))+dot(ahm,jnp.concatenate([bm,bm],0)))+dot(ahm,jnp.concatenate([bh,bh],0))
    return jnp.dot(a,b,precision=lax.Precision.HIGHEST,preferred_element_type=F32)

def sweep(S, first, c0, lane, sub):
    nq=len(S)
    B=[jnp.stack([jnp.broadcast_to(S[q][:,c:c+1],(8,128)) for c in range(c0,c0+SG)]) for q in range(nq)]
    piv=(lane>=c0)&(lane<c0+SG)
    for q in range(nq):
        fill=jnp.where(lane-c0==sub+(8*q-first),1.0,0.0) if first<=8*q<first+SG else 0.0
        S[q]=jnp.where(piv,fill,S[q])
    scale=[None]*nq
    for j in range(SG):
        qj,rj=divmod(first+j,8)
        mine=sub==rj
        inv=1.0/jnp.broadcast_to(B[qj][0,rj:rj+1,:],(8,128))
        rawS=S[qj][rj:rj+1,:]
        g=[(jnp.where(mine,0.0,B[q][0]) if q==qj else B[q][0])*inv for q in range(nq)]
        scale[qj]=inv if scale[qj] is None else jnp.where(sub>=rj,inv,scale[qj])
        if j<SG-1:
            raw=B[qj][1:,rj:rj+1,:]
            B=[B[q][1:]-g[q]*raw for q in range(nq)]
        S=[S[q]-g[q]*rawS for q in range(nq)]
    return [S[q] if scale[q] is None else S[q]*scale[q] for q in range(nq)]

def invert(M, between=None):
    lane=lax.broadcasted_iota(jnp.int32,(8,128),1); sub=lax.broadcasted_iota(jnp.int32,(8,128),0)
    biglane=lax.broadcasted_iota(jnp.int32,(128,128),1)
    def put(rows, start, into):
        return jnp.concatenate([x for x in [into[:start],rows,into[start+rows.shape[0]:]] if x.shape[0]],axis=0)
    zero=jnp.zeros((128,128),F32)
    ahead=[M[8*q:8*q+8,:] for q in range(2)]
    for g in range(8):
        p0=16*g
        if between is not None:
            between(g)
        S=ahead+([M[p0+16+8*q:p0+24+8*q,:] for q in range(2)] if g<7 else [])
        S=sweep(S,0,p0,lane,sub)
        ahead=S[2:]
        R=jnp.concatenate(S[:2],axis=0)
        M=jnp.where((biglane>=p0)&(biglane<p0+16),0.0,M)-mm_inner(M,put(R,p0,zero))
        M=put(R,p0,M)
    return M

def eliminate(mat, between, rest, me):
    for k in range(4):
        b=128*k
        Mi=invert(mat[b:b+128,b:b+128], between if k==0 else None)
        if k==0:
            rest()
        R=mm(Mi,mat[b:b+128,b+128:])
        if k==3:
            mine=pl.ds(pl.multiple_of(me*128,128),128)
            return jnp.where(me==3,R,mat[mine,512:640]-mm(mat[mine,b:b+128],R))
        o=k+1
        mat[128*o:128*o+128,128*o:128*o+128]-=mm(mat[128*o:128*o+128,b:b+128],R[:,:128])
        mat[128*o:128*o+128,128*o+128:]-=mm(mat[128*o:128*o+128,b:b+128],R[:,128:])
        for o in range(4):
            if o not in (k,k+1):
                mat[128*o:128*o+128,b+128:]-=mm(mat[128*o:128*o+128,b:b+128],R)
        mat[b:b+128,b+128:]=R

def assemble(red_ref, last, mat, scale, root, ridge, first):
    r=lax.broadcasted_iota(jnp.int32,(128,128),0); c=lax.broadcasted_iota(jnp.int32,(128,128),1)
    def pair_of(n, diagonal):
        b=red_ref[128*n:128*n+128,:]
        t=b.T
        one=jnp.where(r<=c,b,t); two=jnp.where(r>c,b,jnp.where(r==c,last[diagonal:diagonal+1,:],t))
        return [v*scale+jnp.where(r==c,ridge,0.0) for v in (one,two)]
    if first:
        mat[0:128,0:128]=pair_of(0,4)[0]
        return
    mat[128:256,128:256]=pair_of(0,4)[1]
    mat[256:384,256:384],mat[384:512,384:512]=pair_of(7,5)
    for n,(i,j) in enumerate(CROSS):
        b=red_ref[128*(n+1):128*(n+1)+128,:]*scale
        mat[128*i:128*i+128,128*j:128*j+128]=b
        mat[128*j:128*j+128,128*i:128*i+128]=b.T
    for i in range(4):
        row=last[i:i+1,:]*root
        mat[128*i:128*i+128,512:640]=jnp.broadcast_to(row,(128,128)).T

MESH = pl.DeviceIdType.MESH
RING8 = (4, 3, 5, 2, 6, 1, 7)
OUTWARD = tuple((i,) for i in range(8))
HOMEWARD = ((0, 1), (2, 3, 4, 5, 6, 7))
MIDWAY = 6
LAND = 8


def fit_kernel(dims, consts, bin_hbm, p_hbm, cyc_hbm, az_hbm, src_hbm, out_ref,
               bin_ref, p_ref, cyc_ref, az_ref, src_ref, in_sem, src_scr, mic_scr, hi_scr, lo_scr,
               part, full, mat, last, acc_c, acc_e, acc_x, acc_y, buf_c, buf_ec, buf_x, buf_ex, buf_y, buf_z,
               send_sem, recv_e, recv_c, recv_x, recv_y, recv_z, grecv_y, grecv_x, grecv_c):
    nx, ny, nz, piece = dims
    x = lax.axis_index("grp")
    row = lax.axis_index("row")
    c = lax.rem(row, 2)
    y = lax.rem(row // 2, ny)
    z = row // (2 * ny)

    def at_c():
        return {"row": row + 1 - 2 * c}

    def at_x(o):
        return {"grp": lax.rem(x + o, nx)}

    def at_y(o):
        return {"row": row + 2 * (lax.rem(y + o, ny) - y)}

    def at_z(o):
        return {"row": row + 2 * ny * (lax.rem(z + o, nz) - z)}

    partners = [{"grp": lax.rem(x + o, nx), "row": row + 1 - 2 * c} for o in range(nx)] + [at_x(o) for o in range(1, nx)] + [at_y(o) for o in range(1, ny)]
    partners += [at_z(o) for o in range(1, nz)]
    barrier = pltpu.get_barrier_semaphore()
    for partner in partners:
        pl.semaphore_signal(barrier, inc=1, device_id=partner, device_id_type=MESH)

    loads = []
    for n, (src, dst) in enumerate([(src_hbm, src_ref), (cyc_hbm, cyc_ref), (az_hbm, az_ref), (bin_hbm, bin_ref),
                                    (p_hbm, p_ref)]):
        load = pltpu.make_async_copy(src, dst, in_sem.at[n])
        load.start()
        loads.append(load)
    scale, root, ridge, spacing = consts
    panel_gram(loads, spacing, bin_ref, p_ref, cyc_ref, az_ref, src_ref, part, src_scr, mic_scr, hi_scr, lo_scr)
    pl.semaphore_wait(barrier, len(partners))

    def send(src, dst, ssem, rsem, partner):
        pltpu.make_async_remote_copy(src_ref=src, dst_ref=dst, send_sem=ssem, recv_sem=rsem,
                                     device_id=partner, device_id_type=MESH).start()

    def rows(start, count):
        return pl.ds(pl.multiple_of(start, 8), count)

    def tally(ssem, rsem, count):
        ref = full.at[pl.ds(0, count)]
        return pltpu.make_async_remote_copy(src_ref=ref, dst_ref=ref, send_sem=ssem, recv_sem=rsem,
                                            device_id=at_c(), device_id_type=MESH)

    def arrived(rsem, count):
        tally(send_sem.at[0], rsem, count).wait_recv()

    chunk = piece * nx

    def chunk_of(core, yy):
        return rows((core * ny + yy) * chunk, chunk)

    def piece_of(core, yy, xx):
        return rows(((core * ny + yy) * nx + xx) * piece, piece)

    far = [o for o in RING8 if o < ny] + [0]
    targets = [lax.rem(y + o, ny) for o in far]
    body = chunk * ny * 2
    extra = part.at[pl.ds(body, 8)]
    send(extra, buf_ec, send_sem.at[0], recv_e.at[0], at_c())
    for g, members in enumerate(OUTWARD):
        for i in members:
            send(part.at[chunk_of(1 - c, targets[i])], buf_c.at[i], send_sem.at[0], recv_c.at[g], at_c())
    arrived(recv_e.at[0], 8)
    acc_e[...] = extra[...] + buf_ec[...]
    buf_ex[x] = acc_e[...]
    for o in (2, 1, 3):
        send(acc_e, buf_ex.at[x], send_sem.at[1], recv_e.at[1], at_x(o))
    for g, members in enumerate(OUTWARD):
        arrived(recv_c.at[g], len(members) * chunk)
        for i in members:
            acc_c[i] = part[chunk_of(c, targets[i]), :] + buf_c[i]
        for o in (2, 1, 3):
            for i in members:
                send(acc_c.at[i, rows(lax.rem(x + o, nx) * piece, piece)], buf_x.at[i, o - 1],
                     send_sem.at[1], recv_x.at[g], at_x(o))
    arrived(recv_e.at[1], 8 * (nx - 1))
    spread = buf_ex[0]
    for k in range(1, nx):
        spread = spread + buf_ex[k]
    for g, members in enumerate(OUTWARD):
        arrived(recv_x.at[g], len(members) * piece * (nx - 1))
        for i in members:
            total = acc_c[i, rows(x * piece, piece), :]
            for k in range(nx - 1):
                total = total + buf_x[i, k]
            if far[i]:
                acc_x[i, 0:piece, :] = total
                acc_x[i, piece:piece + 8, :] = spread
                send(acc_x.at[i], buf_y.at[y], send_sem.at[2], recv_y.at[0], at_y(far[i]))
            else:
                buf_y[y, 0:piece, :] = total
                buf_y[y, piece:piece + 8, :] = spread
    wide = piece + 8
    arrived(recv_y.at[0], wide * (ny - 1))
    total = buf_y[0]
    for k in range(1, ny):
        total = total + buf_y[k]
    acc_y[...] = total
    for o in RING8:
        send(acc_y, buf_z.at[z], send_sem.at[3], recv_z.at[0], at_z(o))
    buf_z[z] = total
    arrived(recv_z.at[0], wide * (nz - 1))
    total = buf_z[0]
    for k in range(1, nz):
        total = total + buf_z[k]
    mine = full.at[piece_of(c, y, x)]
    mine[...] = total[0:piece]
    last[...] = total[piece:wide]
    for o in RING8:
        send(mine, mine, send_sem.at[4], grecv_y.at[o - 1], at_y(o))
    early = len(HOMEWARD[0])
    for o in (0,) + RING8[::-1]:
        if o:
            arrived(grecv_y.at[o - 1], piece)
        source = lax.rem(y - o + ny, ny)
        ref = full.at[piece_of(c, source, x)]
        group = (source + ny - early) // ny
        for k in (2, 1, 3):
            send(ref, ref, send_sem.at[5], grecv_x.at[group], at_x(k))

        @pl.when(source < early)
        def _():
            for k in (2, 1, 3, 0):
                across = {"grp": lax.rem(x + k, nx), "row": row + 1 - 2 * c}
                send(ref, ref, send_sem.at[5], grecv_x.at[0], across)

    def to_core(g):
        members = HOMEWARD[g]
        arrived(grecv_x.at[g], len(members) * piece * (nx - 1))
        ref = full.at[rows((c * ny + members[0]) * chunk, len(members) * chunk)]
        send(ref, ref, send_sem.at[6], grecv_c.at[g], at_c())

    def landed(g):
        arrived(grecv_c.at[g], len(HOMEWARD[g]) * chunk)

    arrived(grecv_x.at[0], early * piece * (2 * nx - 1))
    assemble(full, last, mat, scale, root, ridge, True)

    def rest():
        landed(1)
        assemble(full, last, mat, scale, root, ridge, False)

    def between(step):
        if step == MIDWAY:
            to_core(1)
        if step == LAND:
            rest()

    block = eliminate(mat, between, rest if LAND == 8 else lambda: None, x)
    out_ref[...] = block.T[0:1, :]
    for n, count in enumerate((chunk * ny + 8, (piece * ny + 8) * (nx - 1), wide * (ny - 1), wide * (nz - 1), piece * (ny - 1),
                               piece * (ny * (nx - 1) + early * nx), chunk * (ny - early))):
        tally(send_sem.at[n], recv_c.at[0], count).wait_send()


def fit(consts, nx, ny, nz, p, cyc, az, b, src):
    n = p.shape[1]
    rows = 1024
    piece = rows // (2 * nx * ny)
    anywhere = pl.BlockSpec(memory_space=pl.ANY)
    dma = pltpu.SemaphoreType.DMA
    v = pltpu.VMEM

    return pl.pallas_call(
        functools.partial(fit_kernel, (nx, ny, nz, piece), consts),
        out_shape=jax.ShapeDtypeStruct((1, 128), F32),
        in_specs=[anywhere] * 5,
        out_specs=pl.BlockSpec(memory_space=pltpu.VMEM),
        scratch_shapes=[
            pltpu.SMEM((1,), jnp.int32), v((1, n), F32), v((1, n), jnp.int32), v((1, n), jnp.int32),
            v((1, S), jnp.int32), dma((5,)),
            v((S, 128), BF), v((16, n), BF), v((S + 16, n), BF), v((S, n), BF),
            v((rows + 8, 128), F32), v((rows, 128), F32), v((512, 640), F32), v((8, 128), F32),
            v((ny, piece * nx, 128), F32), v((8, 128), F32), v((ny, piece + 8, 128), F32), v((piece + 8, 128), F32),
            v((ny, piece * nx, 128), F32), v((8, 128), F32), v((ny, nx - 1, piece, 128), F32), v((nx, 8, 128), F32),
            v((ny, piece + 8, 128), F32), v((nz, piece + 8, 128), F32),
            dma((7,)), dma((2,)), *[dma((ny,))] * 7,
        ],
        name="fit",
        compiler_params=pltpu.CompilerParams(collective_id=0, has_side_effects=True, vmem_limit_bytes=56 << 20),
    )(b, p, cyc, az, src.reshape(1, S))


def shards(mesh, pressure, mic_cycle, mic_azimuth, bin_index, source_cell):
    nx = mesh.shape["grp"]
    ny = 8
    nz = mesh.shape["row"] // (2 * ny)
    count = pressure.shape[1] * nx * mesh.shape["row"]
    consts = (1.0 / count, 1.0 / count**0.5, 0.5, 0.08)
    return fit(consts, nx, ny, nz, pressure, mic_cycle, mic_azimuth, bin_index, source_cell)


def solution(mesh):
    placed = (P(None, ("grp", "row")), P(None, ("grp", "row")), P(None, ("grp", "row")), P(), P())
    return jax.shard_map(
        functools.partial(shards, mesh), mesh=mesh, in_specs=placed, out_specs=P(None, "grp"), check_vma=False
    )
```

```python
import functools

import jax
import jax.numpy as jnp
import numpy as np
from jax import lax
from jax.experimental import pallas as pl
from jax.experimental.pallas import tpu as pltpu
from jax.sharding import PartitionSpec as P

F32 = jnp.float32
BF = jnp.bfloat16
S = 512
NRING = 4096
NAZ = 8192
CROSS = [(i, j) for i in range(4) for j in range(i + 1, 4)]

NT=(((1,),(1,)),((),()))
CHUNK=256
SINE=(6.283185160089467, -41.341655031414675, 81.60100407316348, -76.54978229140988, 39.5367060495799)
MAGIC=12582912.0

def split(v,n):
    parts=[]
    for _ in range(n-1):
        h=v.astype(BF); parts.append(h); v=v-h.astype(F32)
    parts.append(v.astype(BF)); return parts

def cos_turns(t, gain=None):
    y=t-((t+MAGIC)-MAGIC)
    v=0.25-jnp.abs(y)
    u=v*v
    s=SINE[4]
    for c in SINE[3::-1]: s=s*u+c
    return (s*v) if gain is None else s*(v*gain)

def bf16_parts(value, n):
    parts = []
    for _ in range(n):
        part = float(np.float32(value).astype(jnp.bfloat16))
        parts.append(part)
        value -= part
    return parts


UNIT=bf16_parts((1.5/(2*np.pi))**2, 3)
HALF=256


def order_of(bin_ref):
    order = bin_ref[0].astype(F32) + 1.0
    return order * order


def panel_gram(loads, spacing, bin_ref, p_ref, cyc_ref, az_ref, src_ref, out_ref, src_scr, mic_scr, hi_scr, lo_scr):
    loads[0].wait()
    loads[3].wait()
    cell=src_ref[...].astype(F32)
    li=jnp.floor((cell+0.5)*0.01); rest=cell-100.0*li
    lj=jnp.floor((rest+0.5)*0.1); ll=rest-10.0*lj
    t=[2.0*v-9.0 for v in (li,lj,ll)]
    sq=t[0]*t[0]+t[1]*t[1]+t[2]*t[2]
    one=jnp.ones_like(sq); zero=jnp.zeros_like(sq)
    sq_order=one*(order_of(bin_ref))
    rows=[t[0]]*3+[t[1]]*3+[t[2]]*3+[sq]*3+[sq_order]*3
    sT=jnp.concatenate(rows+[zero]*(128-len(rows)),axis=0)
    src_scr[...]=sT.T.astype(BF)
    loads[1].wait()
    loads[2].wait()
    order=bin_ref[0].astype(F32)+1.0
    turns=(order*order)*float((1.5/(2*np.pi))**2)
    half=spacing*0.5
    polar=(2*cyc_ref[...]+1).astype(F32)*(1.0/16384.0)
    azim=az_ref[...].astype(F32)*(1.0/8192.0)
    sp=cos_turns(polar-0.25); cp=cos_turns(polar)
    mic=[sp*cos_turns(azim), sp*cos_turns(azim-0.25), cp]
    mrows=[]
    for m in mic: mrows+=split(m*(turns*(-2.0*half)),3)
    w=jnp.full(mic[0].shape,half*half,F32)*turns
    mrows+=split(w,3)+[jnp.full(w.shape,v,BF) for v in UNIT]
    mrows=[m.astype(F32) for m in mrows]
    mrows+=[jnp.zeros_like(w)]*(16-len(mrows))
    mic_scr[...]=jnp.concatenate(mrows,axis=0).astype(BF)
    n=p_ref.shape[1]
    loads[4].wait()
    ph,pm=[v.astype(F32) for v in split(p_ref[...],2)]
    hi_scr[HALF:HALF+16,:]=jnp.concatenate([ph,pm]+[jnp.zeros_like(ph)]*14,axis=0).astype(BF)
    def fill(lo, c):
        cols=slice(c*CHUNK,(c+1)*CHUNK)
        t2=jnp.dot(src_scr[lo:lo+HALF,:16],mic_scr[:,cols],preferred_element_type=F32)
        r=lax.rsqrt(t2)
        val=cos_turns(t2*r, r)
        h=val.astype(BF)
        base=lo+(16 if lo else 0)
        hi_scr[base:base+HALF,cols]=h
        lo_scr[lo:lo+HALF,cols]=(val-h.astype(F32)).astype(BF)
    def product(a, b):
        return lax.dot_general(a, b, NT, preferred_element_type=F32)
    R0=HALF+16
    unit=1.5*(bin_ref[0].astype(F32)+1.0)*float(1/(2*np.pi))
    gain=unit*unit
    H1=L1=H2=L2=None
    for c in range(n//CHUNK+1):
        if c<n//CHUNK:
            fill(0, c); fill(HALF, c)
        if c:
            k=slice((c-1)*CHUNK,c*CHUNK)
            new=[product(hi_scr[0:R0,k],hi_scr[0:HALF,k]),product(hi_scr[:,k],lo_scr[0:HALF,k]),product(hi_scr[:,k],hi_scr[R0:,k]),product(hi_scr[:,k],lo_scr[HALF:S,k])]
            if H1 is not None: new=[u+v for u,v in zip((H1,L1,H2,L2),new)]
            H1,L1,H2,L2=new
    def at(i):
        return 128*i+(16 if i>=2 else 0)
    def hblk(i,j):
        m=H1 if j<2 else H2
        return m[at(i):at(i)+128,128*(j%2):128*(j%2)+128]
    def lblk(i,j):
        m=L1 if j<2 else L2
        return m[at(i):at(i)+128,128*(j%2):128*(j%2)+128]
    def gram(i,j):
        return ((hblk(i,j)+lblk(i,j))+lblk(j,i).T)*gain
    ri=lax.broadcasted_iota(jnp.int32,(128,128),0); ci=lax.broadcasted_iota(jnp.int32,(128,128),1)
    diagonals=[]
    for n,i in ((0,0),(7,2)):
        other=gram(i+1,i+1)
        out_ref[128*n:128*n+128,:]=jnp.where(ri<=ci,gram(i,i),other)
        diagonals.append(jnp.sum(jnp.where(ri==ci,other,0.0),axis=0,keepdims=True))
    for n,(i,j) in enumerate(CROSS):
        out_ref[128*(n+1):128*(n+1)+128,:]=gram(i,j)
    r1=(H1[HALF:HALF+1]+L1[HALF:HALF+1])+(H1[HALF+1:HALF+2]+L1[HALF+1:HALF+2])
    r2=(H2[HALF:HALF+1]+L2[HALF:HALF+1])+(H2[HALF+1:HALF+2]+L2[HALF+1:HALF+2])
    tail=jnp.concatenate([r1[:,:128],r1[:,128:],r2[:,:128],r2[:,128:]],axis=0)*unit
    out_ref[1024:1032,:]=jnp.concatenate([tail]+diagonals+[jnp.zeros((2,128),F32)],axis=0)

TERMS=6; INNER=3; SG=16
def dot(a,b): return jnp.dot(a,b,preferred_element_type=F32)
def mm(a,b):
    if TERMS==3:
        ah,am=split(a,2); bh,bm=split(b,2)
        return dot(jnp.concatenate([ah,am],1),jnp.concatenate([bh,bh],0))+dot(ah,bm)
    if TERMS==6:
        ah,am,al=split(a,3); bh,bm,bl_=split(b,3)
        ahm=jnp.concatenate([ah,am],1)
        return (dot(jnp.concatenate([ah,al],1),jnp.concatenate([bl_,bh],0))+dot(ahm,jnp.concatenate([bm,bm],0)))+dot(ahm,jnp.concatenate([bh,bh],0))
    if TERMS==1:
        return dot(a.astype(BF),b.astype(BF))
    return jnp.dot(a,b,precision=lax.Precision.HIGHEST,preferred_element_type=F32)

def bl(v,c): return jnp.broadcast_to(v[:,c:c+1],(8,128))
def bs(v,r): return jnp.broadcast_to(v[r:r+1,:],(8,128))

def mm_inner(a,b):
    if INNER==3:
        ah,am=split(a,2); bh,bm=split(b,2)
        return dot(jnp.concatenate([ah,am],1),jnp.concatenate([bh,bh],0))+dot(ah,bm)
    if INNER==6:
        ah,am,al=split(a,3); bh,bm,bl_=split(b,3)
        ahm=jnp.concatenate([ah,am],1)
        return (dot(jnp.concatenate([ah,al],1),jnp.concatenate([bl_,bh],0))+dot(ahm,jnp.concatenate([bm,bm],0)))+dot(ahm,jnp.concatenate([bh,bh],0))
    return jnp.dot(a,b,precision=lax.Precision.HIGHEST,preferred_element_type=F32)

def sweep(S, first, c0, lane, sub):
    nq=len(S)
    B=[jnp.stack([jnp.broadcast_to(S[q][:,c:c+1],(8,128)) for c in range(c0,c0+SG)]) for q in range(nq)]
    piv=(lane>=c0)&(lane<c0+SG)
    for q in range(nq):
        fill=jnp.where(lane-c0==sub+(8*q-first),1.0,0.0) if first<=8*q<first+SG else 0.0
        S[q]=jnp.where(piv,fill,S[q])
    scale=[None]*nq
    for j in range(SG):
        qj,rj=divmod(first+j,8)
        mine=sub==rj
        inv=1.0/jnp.broadcast_to(B[qj][0,rj:rj+1,:],(8,128))
        rawS=S[qj][rj:rj+1,:]
        g=[(jnp.where(mine,0.0,B[q][0]) if q==qj else B[q][0])*inv for q in range(nq)]
        scale[qj]=inv if scale[qj] is None else jnp.where(sub>=rj,inv,scale[qj])
        if j<SG-1:
            raw=B[qj][1:,rj:rj+1,:]
            B=[B[q][1:]-g[q]*raw for q in range(nq)]
        S=[S[q]-g[q]*rawS for q in range(nq)]
    return [S[q] if scale[q] is None else S[q]*scale[q] for q in range(nq)]

def invert(M, between=None):
    lane=lax.broadcasted_iota(jnp.int32,(8,128),1); sub=lax.broadcasted_iota(jnp.int32,(8,128),0)
    biglane=lax.broadcasted_iota(jnp.int32,(128,128),1)
    def put(rows, start, into):
        return jnp.concatenate([x for x in [into[:start],rows,into[start+rows.shape[0]:]] if x.shape[0]],axis=0)
    zero=jnp.zeros((128,128),F32)
    ahead=[M[8*q:8*q+8,:] for q in range(2)]
    for g in range(8):
        p0=16*g
        if between is not None:
            between(g)
        S=ahead+([M[p0+16+8*q:p0+24+8*q,:] for q in range(2)] if g<7 else [])
        S=sweep(S,0,p0,lane,sub)
        ahead=S[2:]
        R=jnp.concatenate(S[:2],axis=0)
        M=jnp.where((biglane>=p0)&(biglane<p0+16),0.0,M)-mm_inner(M,put(R,p0,zero))
        M=put(R,p0,M)
    return M

def eliminate(mat, between, rest, me):
    for k in range(4):
        b=128*k
        Mi=invert(mat[b:b+128,b:b+128], between if k==0 else None)
        if k==0:
            rest()
        R=mm(Mi,mat[b:b+128,b+128:])
        if k==3:
            mine=pl.ds(pl.multiple_of(me*128,128),128)
            return jnp.where(me==3,R,mat[mine,512:640]-mm(mat[mine,b:b+128],R))
        o=k+1
        mat[128*o:128*o+128,128*o:128*o+128]-=mm(mat[128*o:128*o+128,b:b+128],R[:,:128])
        mat[128*o:128*o+128,128*o+128:]-=mm(mat[128*o:128*o+128,b:b+128],R[:,128:])
        for o in range(4):
            if o not in (k,k+1):
                mat[128*o:128*o+128,b+128:]-=mm(mat[128*o:128*o+128,b:b+128],R)
        mat[b:b+128,b+128:]=R

def assemble(red_ref, last, mat, scale, root, ridge, first):
    r=lax.broadcasted_iota(jnp.int32,(128,128),0); c=lax.broadcasted_iota(jnp.int32,(128,128),1)
    def pair_of(n, diagonal):
        b=red_ref[128*n:128*n+128,:]
        t=b.T
        one=jnp.where(r<=c,b,t); two=jnp.where(r>c,b,jnp.where(r==c,last[diagonal:diagonal+1,:],t))
        return [v*scale+jnp.where(r==c,ridge,0.0) for v in (one,two)]
    if first:
        mat[0:128,0:128]=pair_of(0,4)[0]
        return
    mat[128:256,128:256]=pair_of(0,4)[1]
    mat[256:384,256:384],mat[384:512,384:512]=pair_of(7,5)
    for n,(i,j) in enumerate(CROSS):
        b=red_ref[128*(n+1):128*(n+1)+128,:]*scale
        mat[128*i:128*i+128,128*j:128*j+128]=b
        mat[128*j:128*j+128,128*i:128*i+128]=b.T
    for i in range(4):
        row=last[i:i+1,:]*root
        mat[128*i:128*i+128,512:640]=jnp.broadcast_to(row,(128,128)).T

MESH = pl.DeviceIdType.MESH
RING8 = (4, 3, 5, 2, 6, 1, 7)
OUTWARD = tuple((i,) for i in range(8))
HOMEWARD = ((0, 1), (2, 3, 4, 5, 6, 7))
MIDWAY = 6
LAND = 8


def fit_kernel(dims, consts, bin_hbm, p_hbm, cyc_hbm, az_hbm, src_hbm, out_ref,
               bin_ref, p_ref, cyc_ref, az_ref, src_ref, in_sem, src_scr, mic_scr, hi_scr, lo_scr,
               part, full, mat, last, acc_c, acc_e, acc_x, acc_y, buf_c, buf_ec, buf_x, buf_ex, buf_y, buf_z,
               send_sem, recv_e, recv_c, recv_x, recv_y, recv_z, grecv_y, grecv_x, grecv_c):
    nx, ny, nz, piece = dims
    x = lax.axis_index("grp")
    row = lax.axis_index("row")
    c = lax.rem(row, 2)
    y = lax.rem(row // 2, ny)
    z = row // (2 * ny)

    def at_c():
        return {"row": row + 1 - 2 * c}

    def at_x(o):
        return {"grp": lax.rem(x + o, nx)}

    def at_y(o):
        return {"row": row + 2 * (lax.rem(y + o, ny) - y)}

    def at_z(o):
        return {"row": row + 2 * ny * (lax.rem(z + o, nz) - z)}

    loads = []
    for n, (src, dst) in enumerate([(src_hbm, src_ref), (cyc_hbm, cyc_ref), (az_hbm, az_ref), (bin_hbm, bin_ref),
                                    (p_hbm, p_ref)]):
        load = pltpu.make_async_copy(src, dst, in_sem.at[n])
        load.start()
        loads.append(load)
    partners = [{"grp": lax.rem(x + o, nx), "row": row + 1 - 2 * c} for o in range(nx)] + [at_x(o) for o in range(1, nx)] + [at_y(o) for o in range(1, ny)]
    partners += [at_z(o) for o in range(1, nz)]
    barrier = pltpu.get_barrier_semaphore()
    for partner in partners:
        pl.semaphore_signal(barrier, inc=1, device_id=partner, device_id_type=MESH)

    scale, root, ridge, spacing = consts
    panel_gram(loads, spacing, bin_ref, p_ref, cyc_ref, az_ref, src_ref, part, src_scr, mic_scr, hi_scr, lo_scr)
    pl.semaphore_wait(barrier, len(partners))

    def send(src, dst, ssem, rsem, partner):
        pltpu.make_async_remote_copy(src_ref=src, dst_ref=dst, send_sem=ssem, recv_sem=rsem,
                                     device_id=partner, device_id_type=MESH).start()

    def rows(start, count):
        return pl.ds(pl.multiple_of(start, 8), count)

    def tally(ssem, rsem, count):
        ref = full.at[pl.ds(0, count)]
        return pltpu.make_async_remote_copy(src_ref=ref, dst_ref=ref, send_sem=ssem, recv_sem=rsem,
                                            device_id=at_c(), device_id_type=MESH)

    def arrived(rsem, count):
        tally(send_sem.at[0], rsem, count).wait_recv()

    chunk = piece * nx

    def chunk_of(core, yy):
        return rows((core * ny + yy) * chunk, chunk)

    def piece_of(core, yy, xx):
        return rows(((core * ny + yy) * nx + xx) * piece, piece)

    far = [o for o in RING8 if o < ny] + [0]
    targets = [lax.rem(y + o, ny) for o in far]
    body = chunk * ny * 2
    extra = part.at[pl.ds(body, 8)]
    send(extra, buf_ec, send_sem.at[0], recv_e.at[0], at_c())
    for g, members in enumerate(OUTWARD):
        for i in members:
            send(part.at[chunk_of(1 - c, targets[i])], buf_c.at[i], send_sem.at[0], recv_c.at[g], at_c())
    arrived(recv_e.at[0], 8)
    acc_e[...] = extra[...] + buf_ec[...]
    buf_ex[x] = acc_e[...]
    for o in (2, 1, 3):
        send(acc_e, buf_ex.at[x], send_sem.at[1], recv_e.at[1], at_x(o))
    for g, members in enumerate(OUTWARD):
        arrived(recv_c.at[g], len(members) * chunk)
        for i in members:
            acc_c[i] = part[chunk_of(c, targets[i]), :] + buf_c[i]
        for o in (2, 1, 3):
            for i in members:
                send(acc_c.at[i, rows(lax.rem(x + o, nx) * piece, piece)], buf_x.at[i, o - 1],
                     send_sem.at[1], recv_x.at[g], at_x(o))
    arrived(recv_e.at[1], 8 * (nx - 1))
    spread = buf_ex[0]
    for k in range(1, nx):
        spread = spread + buf_ex[k]
    for g, members in enumerate(OUTWARD):
        arrived(recv_x.at[g], len(members) * piece * (nx - 1))
        for i in members:
            total = acc_c[i, rows(x * piece, piece), :]
            for k in range(nx - 1):
                total = total + buf_x[i, k]
            if far[i]:
                acc_x[i, 0:piece, :] = total
                acc_x[i, piece:piece + 8, :] = spread
                send(acc_x.at[i], buf_y.at[y], send_sem.at[2], recv_y.at[0], at_y(far[i]))
            else:
                buf_y[y, 0:piece, :] = total
                buf_y[y, piece:piece + 8, :] = spread
    wide = piece + 8
    arrived(recv_y.at[0], wide * (ny - 1))
    total = buf_y[0]
    for k in range(1, ny):
        total = total + buf_y[k]
    acc_y[...] = total
    for o in RING8:
        send(acc_y, buf_z.at[z], send_sem.at[3], recv_z.at[0], at_z(o))
    buf_z[z] = total
    arrived(recv_z.at[0], wide * (nz - 1))
    total = buf_z[0]
    for k in range(1, nz):
        total = total + buf_z[k]
    mine = full.at[piece_of(c, y, x)]
    mine[...] = total[0:piece]
    last[...] = total[piece:wide]
    for o in RING8:
        send(mine, mine, send_sem.at[4], grecv_y.at[o - 1], at_y(o))
    early = len(HOMEWARD[0])
    for o in (0,) + RING8[::-1]:
        if o:
            arrived(grecv_y.at[o - 1], piece)
        source = lax.rem(y - o + ny, ny)
        ref = full.at[piece_of(c, source, x)]
        group = (source + ny - early) // ny
        for k in (2, 1, 3):
            send(ref, ref, send_sem.at[5], grecv_x.at[group], at_x(k))

        @pl.when(source < early)
        def _():
            for k in (2, 1, 3, 0):
                across = {"grp": lax.rem(x + k, nx), "row": row + 1 - 2 * c}
                send(ref, ref, send_sem.at[5], grecv_x.at[0], across)

    def to_core(g):
        members = HOMEWARD[g]
        arrived(grecv_x.at[g], len(members) * piece * (nx - 1))
        ref = full.at[rows((c * ny + members[0]) * chunk, len(members) * chunk)]
        send(ref, ref, send_sem.at[6], grecv_c.at[g], at_c())

    def landed(g):
        arrived(grecv_c.at[g], len(HOMEWARD[g]) * chunk)

    arrived(grecv_x.at[0], early * piece * (2 * nx - 1))
    assemble(full, last, mat, scale, root, ridge, True)

    def rest():
        landed(1)
        assemble(full, last, mat, scale, root, ridge, False)

    def between(step):
        if step == MIDWAY:
            to_core(1)
        if step == LAND:
            rest()

    block = eliminate(mat, between, rest if LAND == 8 else lambda: None, x)
    out_ref[...] = block.T[0:1, :]
    for n, count in enumerate((chunk * ny + 8, (piece * ny + 8) * (nx - 1), wide * (ny - 1), wide * (nz - 1), piece * (ny - 1),
                               piece * (ny * (nx - 1) + early * nx), chunk * (ny - early))):
        tally(send_sem.at[n], recv_c.at[0], count).wait_send()


def fit(consts, nx, ny, nz, p, cyc, az, b, src):
    n = p.shape[1]
    rows = 1024
    piece = rows // (2 * nx * ny)
    anywhere = pl.BlockSpec(memory_space=pl.ANY)
    dma = pltpu.SemaphoreType.DMA
    v = pltpu.VMEM

    return pl.pallas_call(
        functools.partial(fit_kernel, (nx, ny, nz, piece), consts),
        out_shape=jax.ShapeDtypeStruct((1, 128), F32),
        in_specs=[anywhere] * 5,
        out_specs=pl.BlockSpec(memory_space=pltpu.VMEM),
        scratch_shapes=[
            pltpu.SMEM((1,), jnp.int32), v((1, n), F32), v((1, n), jnp.int32), v((1, n), jnp.int32),
            v((1, S), jnp.int32), dma((5,)),
            v((S, 128), BF), v((16, n), BF), v((S + 16, n), BF), v((S, n), BF),
            v((rows + 8, 128), F32), v((rows, 128), F32), v((512, 640), F32), v((8, 128), F32),
            v((ny, piece * nx, 128), F32), v((8, 128), F32), v((ny, piece + 8, 128), F32), v((piece + 8, 128), F32),
            v((ny, piece * nx, 128), F32), v((8, 128), F32), v((ny, nx - 1, piece, 128), F32), v((nx, 8, 128), F32),
            v((ny, piece + 8, 128), F32), v((nz, piece + 8, 128), F32),
            dma((7,)), dma((2,)), *[dma((ny,))] * 7,
        ],
        name="fit",
        compiler_params=pltpu.CompilerParams(collective_id=0, has_side_effects=True, vmem_limit_bytes=56 << 20),
    )(b, p, cyc, az, src.reshape(1, S))


def shards(mesh, pressure, mic_cycle, mic_azimuth, bin_index, source_cell):
    nx = mesh.shape["grp"]
    ny = 8
    nz = mesh.shape["row"] // (2 * ny)
    count = pressure.shape[1] * nx * mesh.shape["row"]
    consts = (1.0 / count, 1.0 / count**0.5, 0.5, 0.08)
    return fit(consts, nx, ny, nz, pressure, mic_cycle, mic_azimuth, bin_index, source_cell)


def solution(mesh):
    placed = (P(None, ("grp", "row")), P(None, ("grp", "row")), P(None, ("grp", "row")), P(), P())
    return jax.shard_map(
        functools.partial(shards, mesh), mesh=mesh, in_specs=placed, out_specs=P(None, "grp"), check_vma=False
    )
```

```python
import functools

import jax
import jax.numpy as jnp
import numpy as np
from jax import lax
from jax.experimental import pallas as pl
from jax.experimental.pallas import tpu as pltpu
from jax.sharding import PartitionSpec as P

F32 = jnp.float32
BF = jnp.bfloat16
S = 512
NRING = 4096
NAZ = 8192
CROSS = [(i, j) for i in range(4) for j in range(i + 1, 4)]

NT=(((1,),(1,)),((),()))
CHUNK=256
SINE=(6.283185160089467, -41.341655031414675, 81.60100407316348, -76.54978229140988, 39.5367060495799)
MAGIC=12582912.0

def split(v,n):
    parts=[]
    for _ in range(n-1):
        h=v.astype(BF); parts.append(h); v=v-h.astype(F32)
    parts.append(v.astype(BF)); return parts

def cos_turns(t, gain=None):
    y=t-((t+MAGIC)-MAGIC)
    v=0.25-jnp.abs(y)
    u=v*v
    s=SINE[4]
    for c in SINE[3::-1]: s=s*u+c
    return (s*v) if gain is None else s*(v*gain)

def bf16_parts(value, n):
    parts = []
    for _ in range(n):
        part = float(np.float32(value).astype(jnp.bfloat16))
        parts.append(part)
        value -= part
    return parts


UNIT=bf16_parts((1.5/(2*np.pi))**2, 3)
HALF=256


def order_of(bin_ref):
    order = bin_ref[0].astype(F32) + 1.0
    return order * order


def panel_gram(loads, spacing, bin_ref, p_ref, cyc_ref, az_ref, src_ref, out_ref, src_scr, mic_scr, hi_scr, lo_scr):
    loads[0].wait()
    loads[3].wait()
    cell=src_ref[...].astype(F32)
    li=jnp.floor((cell+0.5)*0.01); rest=cell-100.0*li
    lj=jnp.floor((rest+0.5)*0.1); ll=rest-10.0*lj
    t=[2.0*v-9.0 for v in (li,lj,ll)]
    sq=t[0]*t[0]+t[1]*t[1]+t[2]*t[2]
    one=jnp.ones_like(sq); zero=jnp.zeros_like(sq)
    sq_order=one*(order_of(bin_ref))
    rows=[t[0]]*3+[t[1]]*3+[t[2]]*3+[sq]*3+[sq_order]*3
    sT=jnp.concatenate(rows+[zero]*(128-len(rows)),axis=0)
    src_scr[...]=sT.T.astype(BF)
    loads[1].wait()
    loads[2].wait()
    order=bin_ref[0].astype(F32)+1.0
    turns=(order*order)*float((1.5/(2*np.pi))**2)
    half=spacing*0.5
    polar=(2*cyc_ref[...]+1).astype(F32)*(1.0/16384.0)
    azim=az_ref[...].astype(F32)*(1.0/8192.0)
    sp=cos_turns(polar-0.25); cp=cos_turns(polar)
    mic=[sp*cos_turns(azim), sp*cos_turns(azim-0.25), cp]
    mrows=[]
    for m in mic: mrows+=split(m*(turns*(-2.0*half)),3)
    w=jnp.full(mic[0].shape,half*half,F32)*turns
    mrows+=split(w,3)+[jnp.full(w.shape,v,BF) for v in UNIT]
    mrows=[m.astype(F32) for m in mrows]
    mrows+=[jnp.zeros_like(w)]*(16-len(mrows))
    mic_scr[...]=jnp.concatenate(mrows,axis=0).astype(BF)
    n=p_ref.shape[1]
    loads[4].wait()
    ph,pm=[v.astype(F32) for v in split(p_ref[...],2)]
    hi_scr[HALF:HALF+16,:]=jnp.concatenate([ph,pm]+[jnp.zeros_like(ph)]*14,axis=0).astype(BF)
    def fill(lo, c):
        cols=slice(c*CHUNK,(c+1)*CHUNK)
        t2=jnp.dot(src_scr[lo:lo+HALF,:16],mic_scr[:,cols],preferred_element_type=F32)
        r=lax.rsqrt(t2)
        val=cos_turns(t2*r, r)
        h=val.astype(BF)
        base=lo+(16 if lo else 0)
        hi_scr[base:base+HALF,cols]=h
        lo_scr[lo:lo+HALF,cols]=(val-h.astype(F32)).astype(BF)
    def product(a, b):
        return lax.dot_general(a, b, NT, preferred_element_type=F32)
    R0=HALF+16
    unit=1.5*(bin_ref[0].astype(F32)+1.0)*float(1/(2*np.pi))
    gain=unit*unit
    H1=L1=H2=L2=None
    for c in range(n//CHUNK+1):
        if c<n//CHUNK:
            fill(0, c); fill(HALF, c)
        if c:
            k=slice((c-1)*CHUNK,c*CHUNK)
            new=[product(hi_scr[0:R0,k],hi_scr[0:HALF,k]),product(hi_scr[:,k],lo_scr[0:HALF,k]),product(hi_scr[:,k],hi_scr[R0:,k]),product(hi_scr[:,k],lo_scr[HALF:S,k])]
            if H1 is not None: new=[u+v for u,v in zip((H1,L1,H2,L2),new)]
            H1,L1,H2,L2=new
    def at(i):
        return 128*i+(16 if i>=2 else 0)
    def hblk(i,j):
        m=H1 if j<2 else H2
        return m[at(i):at(i)+128,128*(j%2):128*(j%2)+128]
    def lblk(i,j):
        m=L1 if j<2 else L2
        return m[at(i):at(i)+128,128*(j%2):128*(j%2)+128]
    def gram(i,j):
        return ((hblk(i,j)+lblk(i,j))+lblk(j,i).T)*gain
    ri=lax.broadcasted_iota(jnp.int32,(128,128),0); ci=lax.broadcasted_iota(jnp.int32,(128,128),1)
    diagonals=[]
    for n,i in ((0,0),(7,2)):
        other=gram(i+1,i+1)
        out_ref[128*n:128*n+128,:]=jnp.where(ri<=ci,gram(i,i),other)
        diagonals.append(jnp.sum(jnp.where(ri==ci,other,0.0),axis=0,keepdims=True))
    for n,(i,j) in enumerate(CROSS):
        out_ref[128*(n+1):128*(n+1)+128,:]=gram(i,j)
    r1=(H1[HALF:HALF+1]+L1[HALF:HALF+1])+(H1[HALF+1:HALF+2]+L1[HALF+1:HALF+2])
    r2=(H2[HALF:HALF+1]+L2[HALF:HALF+1])+(H2[HALF+1:HALF+2]+L2[HALF+1:HALF+2])
    tail=jnp.concatenate([r1[:,:128],r1[:,128:],r2[:,:128],r2[:,128:]],axis=0)*unit
    out_ref[1024:1032,:]=jnp.concatenate([tail]+diagonals+[jnp.zeros((2,128),F32)],axis=0)

TERMS=6; INNER=3; SG=16
def dot(a,b): return jnp.dot(a,b,preferred_element_type=F32)
def mm(a,b):
    if TERMS==3:
        ah,am=split(a,2); bh,bm=split(b,2)
        return dot(jnp.concatenate([ah,am],1),jnp.concatenate([bh,bh],0))+dot(ah,bm)
    if TERMS==6:
        ah,am,al=split(a,3); bh,bm,bl_=split(b,3)
        ahm=jnp.concatenate([ah,am],1)
        return (dot(jnp.concatenate([ah,al],1),jnp.concatenate([bl_,bh],0))+dot(ahm,jnp.concatenate([bm,bm],0)))+dot(ahm,jnp.concatenate([bh,bh],0))
    if TERMS==1:
        return dot(a.astype(BF),b.astype(BF))
    return jnp.dot(a,b,precision=lax.Precision.HIGHEST,preferred_element_type=F32)

def bl(v,c): return jnp.broadcast_to(v[:,c:c+1],(8,128))
def bs(v,r): return jnp.broadcast_to(v[r:r+1,:],(8,128))

def mm_inner(a,b):
    if INNER==3:
        ah,am=split(a,2); bh,bm=split(b,2)
        return dot(jnp.concatenate([ah,am],1),jnp.concatenate([bh,bh],0))+dot(ah,bm)
    if INNER==6:
        ah,am,al=split(a,3); bh,bm,bl_=split(b,3)
        ahm=jnp.concatenate([ah,am],1)
        return (dot(jnp.concatenate([ah,al],1),jnp.concatenate([bl_,bh],0))+dot(ahm,jnp.concatenate([bm,bm],0)))+dot(ahm,jnp.concatenate([bh,bh],0))
    return jnp.dot(a,b,precision=lax.Precision.HIGHEST,preferred_element_type=F32)

def sweep(S, first, c0, lane, sub):
    nq=len(S)
    B=[jnp.stack([jnp.broadcast_to(S[q][:,c:c+1],(8,128)) for c in range(c0,c0+SG)]) for q in range(nq)]
    piv=(lane>=c0)&(lane<c0+SG)
    for q in range(nq):
        fill=jnp.where(lane-c0==sub+(8*q-first),1.0,0.0) if first<=8*q<first+SG else 0.0
        S[q]=jnp.where(piv,fill,S[q])
    scale=[None]*nq
    for j in range(SG):
        qj,rj=divmod(first+j,8)
        mine=sub==rj
        inv=1.0/jnp.broadcast_to(B[qj][0,rj:rj+1,:],(8,128))
        rawS=S[qj][rj:rj+1,:]
        g=[(jnp.where(mine,0.0,B[q][0]) if q==qj else B[q][0])*inv for q in range(nq)]
        scale[qj]=inv if scale[qj] is None else jnp.where(sub>=rj,inv,scale[qj])
        if j<SG-1:
            raw=B[qj][1:,rj:rj+1,:]
            B=[B[q][1:]-g[q]*raw for q in range(nq)]
        S=[S[q]-g[q]*rawS for q in range(nq)]
    return [S[q] if scale[q] is None else S[q]*scale[q] for q in range(nq)]

def invert(M, between=None):
    lane=lax.broadcasted_iota(jnp.int32,(8,128),1); sub=lax.broadcasted_iota(jnp.int32,(8,128),0)
    biglane=lax.broadcasted_iota(jnp.int32,(128,128),1)
    def put(rows, start, into):
        return jnp.concatenate([x for x in [into[:start],rows,into[start+rows.shape[0]:]] if x.shape[0]],axis=0)
    zero=jnp.zeros((128,128),F32)
    ahead=[M[8*q:8*q+8,:] for q in range(2)]
    for g in range(8):
        p0=16*g
        if between is not None:
            between(g)
        S=ahead+([M[p0+16+8*q:p0+24+8*q,:] for q in range(2)] if g<7 else [])
        S=sweep(S,0,p0,lane,sub)
        ahead=S[2:]
        R=jnp.concatenate(S[:2],axis=0)
        M=jnp.where((biglane>=p0)&(biglane<p0+16),0.0,M)-mm_inner(M,put(R,p0,zero))
        M=put(R,p0,M)
    return M

def eliminate(mat, between, rest, me):
    for k in range(4):
        b=128*k
        Mi=invert(mat[b:b+128,b:b+128], between if k==0 else None)
        if k==0:
            rest()
        near=mm(Mi,mat[b:b+128,b+128:b+256])
        if k==3:
            mine=pl.ds(pl.multiple_of(me*128,128),128)
            return jnp.where(me==3,near,mat[mine,512:640]-mm(mat[mine,b:b+128],near))
        o=k+1
        mat[128*o:128*o+128,128*o:128*o+128]-=mm(mat[128*o:128*o+128,b:b+128],near)
        away=mm(Mi,mat[b:b+128,b+256:])
        mat[128*o:128*o+128,128*o+128:]-=mm(mat[128*o:128*o+128,b:b+128],away)
        R=jnp.concatenate([near,away],axis=1)
        for o in range(4):
            if o not in (k,k+1):
                mat[128*o:128*o+128,b+128:]-=mm(mat[128*o:128*o+128,b:b+128],R)
        mat[b:b+128,b+128:]=R

def assemble(red_ref, last, mat, scale, root, ridge, first):
    r=lax.broadcasted_iota(jnp.int32,(128,128),0); c=lax.broadcasted_iota(jnp.int32,(128,128),1)
    def pair_of(n, diagonal):
        b=red_ref[128*n:128*n+128,:]
        t=b.T
        one=jnp.where(r<=c,b,t); two=jnp.where(r>c,b,jnp.where(r==c,last[diagonal:diagonal+1,:],t))
        return [v*scale+jnp.where(r==c,ridge,0.0) for v in (one,two)]
    if first:
        mat[0:128,0:128]=pair_of(0,4)[0]
        return
    mat[128:256,128:256]=pair_of(0,4)[1]
    mat[256:384,256:384],mat[384:512,384:512]=pair_of(7,5)
    for n,(i,j) in enumerate(CROSS):
        b=red_ref[128*(n+1):128*(n+1)+128,:]*scale
        mat[128*i:128*i+128,128*j:128*j+128]=b
        mat[128*j:128*j+128,128*i:128*i+128]=b.T
    for i in range(4):
        row=last[i:i+1,:]*root
        mat[128*i:128*i+128,512:640]=jnp.broadcast_to(row,(128,128)).T

MESH = pl.DeviceIdType.MESH
RING8 = (4, 3, 5, 2, 6, 1, 7)
OUTWARD = tuple((i,) for i in range(8))
HOMEWARD = ((0, 1), (2, 3, 4, 5, 6, 7))
MIDWAY = 6
LAND = 8


def fit_kernel(dims, consts, bin_hbm, p_hbm, cyc_hbm, az_hbm, src_hbm, out_ref,
               bin_ref, p_ref, cyc_ref, az_ref, src_ref, in_sem, src_scr, mic_scr, hi_scr, lo_scr,
               part, full, mat, last, acc_c, acc_e, acc_x, acc_y, buf_c, buf_ec, buf_x, buf_ex, buf_y, buf_z,
               send_sem, recv_e, recv_c, recv_x, recv_y, recv_z, grecv_y, grecv_x, grecv_c):
    nx, ny, nz, piece = dims
    x = lax.axis_index("grp")
    row = lax.axis_index("row")
    c = lax.rem(row, 2)
    y = lax.rem(row // 2, ny)
    z = row // (2 * ny)

    def at_c():
        return {"row": row + 1 - 2 * c}

    def at_x(o):
        return {"grp": lax.rem(x + o, nx)}

    def at_y(o):
        return {"row": row + 2 * (lax.rem(y + o, ny) - y)}

    def at_z(o):
        return {"row": row + 2 * ny * (lax.rem(z + o, nz) - z)}

    loads = []
    for n, (src, dst) in enumerate([(src_hbm, src_ref), (cyc_hbm, cyc_ref), (az_hbm, az_ref), (bin_hbm, bin_ref),
                                    (p_hbm, p_ref)]):
        load = pltpu.make_async_copy(src, dst, in_sem.at[n])
        load.start()
        loads.append(load)
    partners = [{"grp": lax.rem(x + o, nx), "row": row + 1 - 2 * c} for o in range(nx)] + [at_x(o) for o in range(1, nx)] + [at_y(o) for o in range(1, ny)]
    partners += [at_z(o) for o in range(1, nz)]
    barrier = pltpu.get_barrier_semaphore()
    for partner in partners:
        pl.semaphore_signal(barrier, inc=1, device_id=partner, device_id_type=MESH)

    scale, root, ridge, spacing = consts
    panel_gram(loads, spacing, bin_ref, p_ref, cyc_ref, az_ref, src_ref, part, src_scr, mic_scr, hi_scr, lo_scr)
    pl.semaphore_wait(barrier, len(partners))

    def send(src, dst, ssem, rsem, partner):
        pltpu.make_async_remote_copy(src_ref=src, dst_ref=dst, send_sem=ssem, recv_sem=rsem,
                                     device_id=partner, device_id_type=MESH).start()

    def rows(start, count):
        return pl.ds(pl.multiple_of(start, 8), count)

    def tally(ssem, rsem, count):
        ref = full.at[pl.ds(0, count)]
        return pltpu.make_async_remote_copy(src_ref=ref, dst_ref=ref, send_sem=ssem, recv_sem=rsem,
                                            device_id=at_c(), device_id_type=MESH)

    def arrived(rsem, count):
        tally(send_sem.at[0], rsem, count).wait_recv()

    chunk = piece * nx

    def chunk_of(core, yy):
        return rows((core * ny + yy) * chunk, chunk)

    def piece_of(core, yy, xx):
        return rows(((core * ny + yy) * nx + xx) * piece, piece)

    far = [o for o in RING8 if o < ny] + [0]
    targets = [lax.rem(y + o, ny) for o in far]
    body = chunk * ny * 2
    extra = part.at[pl.ds(body, 8)]
    send(extra, buf_ec, send_sem.at[0], recv_e.at[0], at_c())
    for g, members in enumerate(OUTWARD):
        for i in members:
            send(part.at[chunk_of(1 - c, targets[i])], buf_c.at[i], send_sem.at[0], recv_c.at[g], at_c())
    arrived(recv_e.at[0], 8)
    acc_e[...] = extra[...] + buf_ec[...]
    buf_ex[x] = acc_e[...]
    for o in (2, 1, 3):
        send(acc_e, buf_ex.at[x], send_sem.at[1], recv_e.at[1], at_x(o))
    for g, members in enumerate(OUTWARD):
        arrived(recv_c.at[g], len(members) * chunk)
        for i in members:
            acc_c[i] = part[chunk_of(c, targets[i]), :] + buf_c[i]
        for o in (2, 1, 3):
            for i in members:
                send(acc_c.at[i, rows(lax.rem(x + o, nx) * piece, piece)], buf_x.at[i, o - 1],
                     send_sem.at[1], recv_x.at[g], at_x(o))
    arrived(recv_e.at[1], 8 * (nx - 1))
    spread = buf_ex[0]
    for k in range(1, nx):
        spread = spread + buf_ex[k]
    for g, members in enumerate(OUTWARD):
        arrived(recv_x.at[g], len(members) * piece * (nx - 1))
        for i in members:
            total = acc_c[i, rows(x * piece, piece), :]
            for k in range(nx - 1):
                total = total + buf_x[i, k]
            if far[i]:
                acc_x[i, 0:piece, :] = total
                acc_x[i, piece:piece + 8, :] = spread
                send(acc_x.at[i], buf_y.at[y], send_sem.at[2], recv_y.at[0], at_y(far[i]))
            else:
                buf_y[y, 0:piece, :] = total
                buf_y[y, piece:piece + 8, :] = spread
    wide = piece + 8
    arrived(recv_y.at[0], wide * (ny - 1))
    total = buf_y[0]
    for k in range(1, ny):
        total = total + buf_y[k]
    acc_y[...] = total
    for o in RING8:
        send(acc_y, buf_z.at[z], send_sem.at[3], recv_z.at[0], at_z(o))
    buf_z[z] = total
    arrived(recv_z.at[0], wide * (nz - 1))
    total = buf_z[0]
    for k in range(1, nz):
        total = total + buf_z[k]
    mine = full.at[piece_of(c, y, x)]
    mine[...] = total[0:piece]
    last[...] = total[piece:wide]
    for o in RING8:
        send(mine, mine, send_sem.at[4], grecv_y.at[o - 1], at_y(o))
    early = len(HOMEWARD[0])
    for o in (0,) + RING8[::-1]:
        if o:
            arrived(grecv_y.at[o - 1], piece)
        source = lax.rem(y - o + ny, ny)
        ref = full.at[piece_of(c, source, x)]
        group = (source + ny - early) // ny
        for k in (2, 1, 3):
            send(ref, ref, send_sem.at[5], grecv_x.at[group], at_x(k))

        @pl.when(source < early)
        def _():
            for k in (2, 1, 3, 0):
                across = {"grp": lax.rem(x + k, nx), "row": row + 1 - 2 * c}
                send(ref, ref, send_sem.at[5], grecv_x.at[0], across)

    def to_core(g):
        members = HOMEWARD[g]
        arrived(grecv_x.at[g], len(members) * piece * (nx - 1))
        ref = full.at[rows((c * ny + members[0]) * chunk, len(members) * chunk)]
        send(ref, ref, send_sem.at[6], grecv_c.at[g], at_c())

    def landed(g):
        arrived(grecv_c.at[g], len(HOMEWARD[g]) * chunk)

    arrived(grecv_x.at[0], early * piece * (2 * nx - 1))
    assemble(full, last, mat, scale, root, ridge, True)

    def rest():
        landed(1)
        assemble(full, last, mat, scale, root, ridge, False)

    def between(step):
        if step == MIDWAY:
            to_core(1)
        if step == LAND:
            rest()

    block = eliminate(mat, between, rest if LAND == 8 else lambda: None, x)
    out_ref[...] = block.T[0:1, :]
    for n, count in enumerate((chunk * ny + 8, (piece * ny + 8) * (nx - 1), wide * (ny - 1), wide * (nz - 1), piece * (ny - 1),
                               piece * (ny * (nx - 1) + early * nx), chunk * (ny - early))):
        tally(send_sem.at[n], recv_c.at[0], count).wait_send()


def fit(consts, nx, ny, nz, p, cyc, az, b, src):
    n = p.shape[1]
    rows = 1024
    piece = rows // (2 * nx * ny)
    anywhere = pl.BlockSpec(memory_space=pl.ANY)
    dma = pltpu.SemaphoreType.DMA
    v = pltpu.VMEM

    return pl.pallas_call(
        functools.partial(fit_kernel, (nx, ny, nz, piece), consts),
        out_shape=jax.ShapeDtypeStruct((1, 128), F32),
        in_specs=[anywhere] * 5,
        out_specs=pl.BlockSpec(memory_space=pltpu.VMEM),
        scratch_shapes=[
            pltpu.SMEM((1,), jnp.int32), v((1, n), F32), v((1, n), jnp.int32), v((1, n), jnp.int32),
            v((1, S), jnp.int32), dma((5,)),
            v((S, 128), BF), v((16, n), BF), v((S + 16, n), BF), v((S, n), BF),
            v((rows + 8, 128), F32), v((rows, 128), F32), v((512, 640), F32), v((8, 128), F32),
            v((ny, piece * nx, 128), F32), v((8, 128), F32), v((ny, piece + 8, 128), F32), v((piece + 8, 128), F32),
            v((ny, piece * nx, 128), F32), v((8, 128), F32), v((ny, nx - 1, piece, 128), F32), v((nx, 8, 128), F32),
            v((ny, piece + 8, 128), F32), v((nz, piece + 8, 128), F32),
            dma((7,)), dma((2,)), *[dma((ny,))] * 7,
        ],
        name="fit",
        compiler_params=pltpu.CompilerParams(collective_id=0, has_side_effects=True, vmem_limit_bytes=56 << 20),
    )(b, p, cyc, az, src.reshape(1, S))


def shards(mesh, pressure, mic_cycle, mic_azimuth, bin_index, source_cell):
    nx = mesh.shape["grp"]
    ny = 8
    nz = mesh.shape["row"] // (2 * ny)
    count = pressure.shape[1] * nx * mesh.shape["row"]
    consts = (1.0 / count, 1.0 / count**0.5, 0.5, 0.08)
    return fit(consts, nx, ny, nz, pressure, mic_cycle, mic_azimuth, bin_index, source_cell)


def solution(mesh):
    placed = (P(None, ("grp", "row")), P(None, ("grp", "row")), P(None, ("grp", "row")), P(), P())
    return jax.shard_map(
        functools.partial(shards, mesh), mesh=mesh, in_specs=placed, out_specs=P(None, "grp"), check_vma=False
    )
```
